32 devices in a mesh: qrow: 2 (over x), kcol: 16 (over z, y, core).
Axes of the slice: x: 2, y: 2, z: 4, core: 2. Of those that a mesh axis runs over, the one named last changes fastest.
Arguments:
- queries: bfloat16 [32, 2048], P(('qrow', 'kcol')), may hold values from -96 to 96, as said below
- key_maps: bfloat16 [8192, 2048], P(('qrow', 'kcol')), may hold values from -4.1 to 4.1, as said below
- values: bfloat16 [8192, 2048], P(('qrow', 'kcol')), may hold values from -24 to 24
- lambdas: float32 [8], replicated, may hold values from 0.2 to 0.8
- norm_gain: float32 [2048], replicated, may hold values from 0.1 to 1.9
Outputs:
- attended: bfloat16 [32, 2048], P(('qrow', 'kcol'))
The draws below stay inside these ranges and needn't reach their ends.
Inputs may be any that keep to these rules, and one draw needn't show every extreme that they name: `queries`: query features of order one in most rows. `key_maps`: key features of order one.
All inputs are finite; a program needn't handle non-finite values.
Results may differ from the reference program's by a relative error of at most 0.014.
Values may be sent and summed in bfloat16 or wider, within the bound.
A program may use at most 64 MiB of HBM per device.

```python
import math
import jax
import jax.numpy as jnp
from jax import lax

HEADS = 8
HD = 128
VD = 256
Q = 32
CTX = 8192
N_QROW = 2


def shared_keys(key):
    return jnp.clip(jax.random.normal(key, (CTX, 2 * HEADS * HD), jnp.float32), -4.0, 4.0)


def draw_key_maps(key, part):
    base = shared_keys(key)
    return base.astype(jnp.bfloat16)


def draw_queries(key, part):
    key = jax.random.fold_in(key, 2)
    result = jnp.clip(1.6 * jax.random.normal(key, (Q, 2 * HEADS * HD), jnp.float32), -6.4, 6.4)
    return result.astype(jnp.bfloat16)


def steps_of(key, dims, cuts, least, high):
    factor_of, own = 1.0, jax.random.fold_in(key, 6)
    for position, parts in cuts:
        draws = jnp.exp(jax.random.uniform(jax.random.fold_in(own, position), (parts,), jnp.float32, least / len(cuts), high / len(cuts)))
        factor_of = factor_of * jnp.repeat(draws, dims[position] // parts).reshape([-1 if axis == position else 1 for axis in range(len(dims))])
    return factor_of


def normal_values(stream_key, shape, width, reach, shards=(), held_as=jnp.bfloat16):
    drawn = width * jax.random.normal(stream_key, shape, jnp.float32)
    if shards:
        drawn = drawn * steps_of(stream_key, shape, shards, -0.22, 0.18)
    return jnp.clip(drawn, -reach, reach).astype(held_as)


def setup_inputs(seed: int = 0) -> dict:
    seeds = jax.random.split(jax.random.key(seed), 6)
    return {
        "queries": draw_queries(jax.random.fold_in(seeds[5], 71), 0),
        "key_maps": draw_key_maps(jax.random.fold_in(seeds[5], 71), 0),
        "values": normal_values(seeds[2], (CTX, HEADS * VD), 4.0, 24.0, ((0, 32),)),
        "lambdas": jnp.clip(jax.random.uniform(seeds[3], (HEADS,), jnp.float32, 0.2, 0.8), 0.2, 0.8),
        "norm_gain": jnp.clip(1.0 + 0.18 * jax.random.normal(seeds[4], (HEADS * VD,), jnp.float32), 0.1, 1.9),
    }


def reference(queries, key_maps, values, lambdas, norm_gain):
    scaling = 1.0 / math.sqrt(HD)
    per_block = Q // N_QROW
    block_count = Q // per_block
    key_heads = key_maps.reshape(CTX, HEADS, 2, HD).transpose(1, 2, 0, 3)
    value_heads = values.reshape(CTX, HEADS, VD).transpose(1, 0, 2)
    query_blocks = queries.reshape(block_count, per_block, HEADS, 2, HD).transpose(0, 2, 3, 1, 4)
    key_pos = jnp.arange(CTX, dtype=jnp.int32)
    starts = (jnp.arange(block_count, dtype=jnp.int32) * per_block).astype(jnp.int32)

    def one_block(inputs):
        query_heads, first = inputs
        query_pos = (CTX - Q + first + jnp.arange(per_block, dtype=jnp.int32)).astype(jnp.int32)
        visible = key_pos[None, :] <= query_pos[:, None]

        def one_head(head_inputs):
            query_pair, key_pair, value_rows, weight_two = head_inputs
            outputs = []
            for map_side in range(2):
                score = jnp.dot(query_pair[map_side], key_pair[map_side].T, preferred_element_type=jnp.float32) * scaling
                score = jnp.where(visible, score, -1e+30)
                largest = lax.optimization_barrier(jnp.max(score, axis=1))
                expo = jnp.where(visible, jnp.exp(score - largest[:, None]), 0.0)
                total = lax.optimization_barrier(jnp.sum(expo, axis=1))
                summed = jnp.dot(expo.astype(jnp.bfloat16), value_rows, preferred_element_type=jnp.float32)
                outputs.append(summed / total[:, None])
            return outputs[0] - weight_two * outputs[1]
        return lax.map(one_head, (query_heads, key_heads, value_heads, lambdas))
    diffs = lax.map(one_block, (query_blocks, starts))
    diffs = diffs.transpose(0, 2, 1, 3).reshape(Q, HEADS, VD)
    meansq = lax.optimization_barrier(jnp.mean(diffs * diffs, axis=-1, keepdims=True))
    normed = diffs / jnp.sqrt(meansq + 1e-05) * norm_gain.reshape(HEADS, VD)
    return normed.reshape(Q, HEADS * VD).astype(jnp.bfloat16)
```

```python
import functools
import math

import jax
import jax.numpy as jnp
from jax import lax
from jax.experimental import pallas as pl
from jax.experimental.pallas import tpu as pltpu
from jax.sharding import PartitionSpec as P

MESH = pl.DeviceIdType.MESH
LOWEST = -1e30


def kernel(
    rows, cols, key_dev, heads,
    q_hbm, k_hbm, v_hbm, lam_ref, gain_hbm,
    out_ref,
    q_own, gain_own, k_buf, v_buf, q_split, q_pair, q_all, q_wide,
    part_wide, part_send, part_recv, diff_pad, gain_rows, fin_send, fin_recv,
    q_sem, gain_sem, k_own_sem, v_own_sem, k_send, k_recv, v_send, v_recv,
    qx_send, qx_recv, qa_send, qa_recv, pa_send, pa_recv, fx_send, fx_recv,
):
    row = lax.axis_index("qrow")
    col = lax.axis_index("kcol")
    core = lax.rem(col, 2)
    half_cols = cols // 2
    pairs = rows * half_cols
    pair = row * half_cols + lax.div(col, 2)
    sib = (row, col + 1 - 2 * core)
    group = heads // 2
    maps = 2 * group
    width = group * 256
    tall = 2 * pairs

    def peer(offset):
        other = lax.rem(pair + offset, pairs)
        return (lax.div(other, half_cols), 2 * lax.rem(other, half_cols) + core)

    def columns(which, h):
        return pl.ds(pl.multiple_of(which * width + h * 256, 128), 256)

    q_copy = pltpu.make_async_copy(q_hbm, q_own, q_sem)
    q_copy.start()
    gain_copy = pltpu.make_async_copy(gain_hbm, gain_own, gain_sem)
    gain_copy.start()
    k_locals, v_locals = [], []
    for h in range(group):
        k_locals.append(pltpu.make_async_copy(
            k_hbm.at[:, columns(core, h)], k_buf.at[h, pl.ds(0, key_dev)], k_own_sem.at[h]))
        k_locals[-1].start()
    for h in range(group):
        v_locals.append(pltpu.make_async_copy(
            v_hbm.at[:, columns(core, h)], v_buf.at[h, pl.ds(0, key_dev)], v_own_sem.at[h]))
        v_locals[-1].start()

    barrier = pltpu.get_barrier_semaphore()
    pl.semaphore_signal(barrier, inc=1, device_id=sib, device_id_type=MESH)

    def greet(i, carry):
        pl.semaphore_signal(barrier, inc=1, device_id=peer(i), device_id_type=MESH)
        return carry

    lax.fori_loop(1, pairs, greet, 0)

    q_copy.wait()
    for g in range(2):
        for m in range(maps):
            at = (g * maps + m) * 128
            q_split[g, m : m + 1, :] = q_own[:, at : at + 128].astype(jnp.float32)
    q_pair[core] = q_split[core]

    pl.semaphore_wait(barrier, pairs)

    q_cross = pltpu.make_async_remote_copy(
        src_ref=q_split.at[1 - core], dst_ref=q_pair.at[core], send_sem=qx_send, recv_sem=qx_recv,
        device_id=sib, device_id_type=MESH)
    q_cross.start()
    k_cross, v_cross = [], []
    for h in range(group):
        k_cross.append(pltpu.make_async_remote_copy(
            src_ref=k_hbm.at[:, columns(1 - core, h)], dst_ref=k_buf.at[h, pl.ds(key_dev, key_dev)],
            send_sem=k_send.at[h], recv_sem=k_recv.at[h], device_id=sib, device_id_type=MESH))
        k_cross[-1].start()
    for h in range(group):
        v_cross.append(pltpu.make_async_remote_copy(
            src_ref=v_hbm.at[:, columns(1 - core, h)], dst_ref=v_buf.at[h, pl.ds(key_dev, key_dev)],
            send_sem=v_send.at[h], recv_sem=v_recv.at[h], device_id=sib, device_id_type=MESH))
        v_cross[-1].start()

    q_cross.wait_recv()
    q_all[0] = q_pair[...].reshape(2 * maps, 128).astype(jnp.bfloat16)

    def send_query(i, carry):
        pltpu.make_async_remote_copy(
            src_ref=q_all.at[0], dst_ref=q_all.at[pairs - i], send_sem=qa_send, recv_sem=qa_recv,
            device_id=peer(i), device_id_type=MESH).start()
        return carry

    lax.fori_loop(1, pairs, send_query, 0)

    gain_copy.wait()
    for part in range(2):
        for h in range(group):
            line = gain_own[pl.ds((core * group + h) * 2 + part, 1), :]
            gain_rows[part, h : h + 1, :] = line
            gain_rows[part, group + h : group + h + 1, :] = line
    line_of = lax.rem(lax.broadcasted_iota(jnp.int32, (2 * group, 128), 0), group)
    lam = jnp.zeros((2 * group, 128), jnp.float32)
    for h in range(group):
        lam = jnp.where(line_of == h, lam_ref[core * group + h], lam)

    keys = 2 * key_dev
    row_of = lax.broadcasted_iota(jnp.int32, (tall, keys), 0)
    col_of = lax.broadcasted_iota(jnp.int32, (tall, keys), 1)
    query = 2 * pair + row_of
    query = jnp.where(query >= tall, query - tall, query)
    block = jnp.where(col_of < key_dev, 2 * pair + core, 2 * pair + 1 - core)
    place = jnp.where(col_of < key_dev, col_of, col_of - key_dev)
    visible = block * key_dev + place <= tall * key_dev - tall + query
    lane = lax.broadcasted_iota(jnp.int32, (tall, 128), 1)
    scaling = 1.0 / math.sqrt(128)

    pltpu.make_async_copy(q_all.at[pl.ds(1, pairs - 1)], q_all.at[pl.ds(1, pairs - 1)], qa_recv).wait()
    q_wide[...] = q_all[...].reshape(pairs * 2 * maps, 128).astype(jnp.float32)

    for h in range(group):
        k_locals[h].wait()
        k_cross[h].wait_recv()
        expos = []
        for side in range(2):
            m = 2 * h + side
            q_map = q_wide[pl.ds(m, tall, stride=maps), :].astype(jnp.bfloat16)
            score = lax.dot_general(
                q_map, k_buf[h, :, side * 128 : side * 128 + 128], (((1,), (1,)), ((), ())),
                preferred_element_type=jnp.float32) * scaling
            score = jnp.where(visible, score, LOWEST)
            top = jnp.max(score, axis=1, keepdims=True).astype(jnp.bfloat16).astype(jnp.float32)
            expo = jnp.where(visible, jnp.exp(score - top), 0.0)
            total = jnp.sum(expo, axis=1, keepdims=True)
            high = total.astype(jnp.bfloat16).astype(jnp.float32)
            stats = jnp.where(lane == 0, top, jnp.where(lane == 1, high, total - high))
            part_wide[2, pl.ds(m, tall, stride=maps), :] = stats
            expos.append(expo.astype(jnp.bfloat16))
        v_locals[h].wait()
        v_cross[h].wait_recv()
        summed = jnp.dot(jnp.concatenate(expos, axis=0), v_buf[h], preferred_element_type=jnp.float32)
        for side in range(2):
            for part in range(2):
                part_wide[part, pl.ds(2 * h + side, tall, stride=maps), :] = summed[
                    side * tall : (side + 1) * tall, part * 128 : part * 128 + 128]

    for part in range(3):
        part_send[:, part] = part_wide[part].reshape(pairs, 2 * maps, 128).astype(jnp.bfloat16)

    def send_part(i, carry):
        pltpu.make_async_remote_copy(
            src_ref=part_send.at[i], dst_ref=part_recv.at[i], send_sem=pa_send, recv_sem=pa_recv,
            device_id=peer(i), device_id_type=MESH).start()
        return carry

    lax.fori_loop(1, pairs, send_part, 0)
    part_recv[0] = part_send[0]
    pltpu.make_async_copy(
        part_recv.at[pl.ds(1, pairs - 1)], part_recv.at[pl.ds(1, pairs - 1)], pa_recv).wait()

    stats_all = part_recv[:, 2].astype(jnp.float32)
    peak = jnp.max(stats_all, axis=0)
    shape = (2 * maps, 128)
    sums = [jnp.zeros(shape, jnp.float32) for _ in range(3)]
    for s in range(pairs):
        factor = jnp.broadcast_to(jnp.exp(stats_all[s] - peak)[:, 0:1], shape)
        for part in range(3):
            sums[part] = sums[part] + factor * part_recv[s, part].astype(jnp.float32)
    totals = sums[2][:, 1:2] + sums[2][:, 2:3]
    diffs = []
    for part in range(2):
        diff_pad[part] = sums[part] / totals
        diffs.append(
            diff_pad[part, pl.ds(0, maps, stride=2), :] - lam * diff_pad[part, pl.ds(1, maps, stride=2), :])
    square = jnp.sum(diffs[0] * diffs[0] + diffs[1] * diffs[1], axis=1, keepdims=True) * (1.0 / 256)
    scale = jnp.sqrt(square + 1e-05)
    for part in range(2):
        normed = diffs[part] / scale * gain_rows[part]
        for j in range(2):
            fin_send[j, part * group : (part + 1) * group, :] = normed[j * group : (j + 1) * group]
    fin_cross = pltpu.make_async_remote_copy(
        src_ref=fin_send.at[1 - core], dst_ref=fin_recv, send_sem=fx_send, recv_sem=fx_recv,
        device_id=sib, device_id_type=MESH)
    fin_cross.start()

    def put(which, lines):
        for part in range(2):
            for h in range(group):
                at = pl.ds(pl.multiple_of(which * width + h * 256 + part * 128, 128), 128)
                out_ref[:, at] = lines[part * group + h : part * group + h + 1]

    put(core, fin_send[core])
    q_cross.wait_send()
    for h in range(group):
        k_cross[h].wait_send()
        v_cross[h].wait_send()
    pltpu.make_async_copy(q_all.at[pl.ds(1, pairs - 1)], q_all.at[pl.ds(1, pairs - 1)], qa_send).wait()
    pltpu.make_async_copy(
        part_send.at[pl.ds(1, pairs - 1)], part_send.at[pl.ds(1, pairs - 1)], pa_send).wait()
    fin_cross.wait()
    put(1 - core, fin_recv[...])


def shards(queries, key_maps, values, lambdas, norm_gain):
    rows, cols = lax.axis_size("qrow"), lax.axis_size("kcol")
    heads = lambdas.shape[0]
    key_dev = key_maps.shape[0]
    assert queries.shape[0] == 1 and heads == 8
    assert key_maps.shape[1] == 2048 and values.shape[1] == 2048
    assert cols % 2 == 0
    group = heads // 2
    maps = 2 * group
    pairs = rows * cols // 2
    tall = 2 * pairs
    f32, bf16 = jnp.float32, jnp.bfloat16
    dma = pltpu.SemaphoreType.DMA
    anywhere = pl.BlockSpec(memory_space=pl.ANY)
    out = pl.pallas_call(
        functools.partial(kernel, rows, cols, key_dev, heads),
        out_shape=jax.ShapeDtypeStruct((1, 2048), f32),
        in_specs=[anywhere, anywhere, anywhere, pl.BlockSpec(memory_space=pltpu.SMEM), anywhere],
        out_specs=pl.BlockSpec(memory_space=pltpu.VMEM),
        scratch_shapes=[
            pltpu.VMEM((1, 2048), bf16),
            pltpu.VMEM((16, 128), f32),
            pltpu.VMEM((group, 2 * key_dev, 256), bf16),
            pltpu.VMEM((group, 2 * key_dev, 256), bf16),
            pltpu.VMEM((2, maps, 128), f32),
            pltpu.VMEM((2, maps, 128), f32),
            pltpu.VMEM((pairs, 2 * maps, 128), bf16),
            pltpu.VMEM((pairs * 2 * maps, 128), f32),
            pltpu.VMEM((3, pairs * 2 * maps, 128), f32),
            pltpu.VMEM((pairs, 3, 2 * maps, 128), bf16),
            pltpu.VMEM((pairs, 3, 2 * maps, 128), bf16),
            pltpu.VMEM((2, 2 * maps, 128), f32),
            pltpu.VMEM((2, 2 * group, 128), f32),
            pltpu.VMEM((2, 2 * group, 128), f32),
            pltpu.VMEM((2 * group, 128), f32),
            dma, dma, dma((group,)), dma((group,)), dma((group,)), dma((group,)), dma((group,)), dma((group,)),
            dma, dma, dma, dma, dma, dma, dma, dma,
        ],
        compiler_params=pltpu.CompilerParams(
            collective_id=0, has_side_effects=True, vmem_limit_bytes=40 * 2**20),
        cost_estimate=pl.CostEstimate(
            flops=6 * tall * 2 * key_dev * 1024, bytes_accessed=4 * key_dev * 2048, transcendentals=0),
    )(queries, key_maps, values, lambdas, norm_gain.reshape(16, 128))
    return out.astype(bf16)


def solution(mesh):
    in_specs = (
        P(("qrow", "kcol"), None),
        P(("qrow", "kcol"), None),
        P(("qrow", "kcol"), None),
        P(),
        P(),
    )
    out_specs = P(("qrow", "kcol"), None)
    return jax.shard_map(shards, mesh=mesh, in_specs=in_specs, out_specs=out_specs, check_vma=False)
```

```python
import functools
import math

import jax
import jax.numpy as jnp
from jax import lax
from jax.experimental import pallas as pl
from jax.experimental.pallas import tpu as pltpu
from jax.sharding import PartitionSpec as P

MESH = pl.DeviceIdType.MESH
LOWEST = -1e30


def kernel(
    rows, cols, key_dev, heads,
    q_hbm, k_hbm, v_hbm, lam_hbm, gain_hbm,
    out_ref,
    q_own, lam_own, gain_own, k_buf, v_buf, q_split, q_pair, q_all, q_wide, bias,
    stat_send, stat_recv, part_wide, part_send, part_recv, sum_pad, gain_rows, fin_send, fin_recv,
    q_sem, lam_sem, gain_sem, k_own_sem, v_own_sem, k_send, k_recv, v_send, v_recv,
    qx_send, qx_recv, qa_send, qa_recv, st_send, st_recv, pa_send, pa_recv, fx_send, fx_recv,
):
    row = lax.axis_index("qrow")
    col = lax.axis_index("kcol")
    core = lax.rem(col, 2)
    half_cols = cols // 2
    pairs = rows * half_cols
    pair = row * half_cols + lax.div(col, 2)
    sib = (row, col + 1 - 2 * core)
    group = heads // 2
    maps = 2 * group
    width = group * 256
    tall = 2 * pairs
    keys = 2 * key_dev

    def peer(offset):
        other = pair + offset
        other = jnp.where(other >= pairs, other - pairs, other)
        its_row = lax.div(other, half_cols)
        return (its_row, 2 * (other - its_row * half_cols) + core)

    def for_peers(step):
        if pairs <= 16:
            for i in range(1, pairs):
                step(i)
        else:
            lax.fori_loop(1, pairs, lambda i, carry: (step(i), carry)[1], 0)

    def columns(which, h):
        return pl.ds(pl.multiple_of(which * width + h * 256, 128), 256)

    def all_of(ref, sem):
        pltpu.make_async_copy(ref, ref, sem).wait()

    q_copy = pltpu.make_async_copy(q_hbm, q_own, q_sem)
    q_copy.start()
    barrier = pltpu.get_barrier_semaphore()
    for_peers(lambda i: pl.semaphore_signal(barrier, inc=1, device_id=peer(i), device_id_type=MESH))
    pl.semaphore_signal(barrier, inc=1, device_id=sib, device_id_type=MESH)

    lam_copy = pltpu.make_async_copy(lam_hbm, lam_own, lam_sem)
    lam_copy.start()
    gain_copy = pltpu.make_async_copy(gain_hbm, gain_own, gain_sem)
    gain_copy.start()
    k_locals, v_locals = [], []
    for h in range(group):
        k_locals.append(pltpu.make_async_copy(
            k_hbm.at[:, columns(core, h)], k_buf.at[h, pl.ds(0, key_dev)], k_own_sem.at[h]))
        k_locals[-1].start()
    for h in range(group):
        v_locals.append(pltpu.make_async_copy(
            v_hbm.at[:, columns(core, h)], v_buf.at[h, pl.ds(0, key_dev)], v_own_sem.at[h]))
        v_locals[-1].start()

    q_copy.wait()
    for g in range(2):
        for m in range(maps):
            at = (g * maps + m) * 128
            q_split[g, m : m + 1, :] = q_own[:, at : at + 128].astype(jnp.float32)
    q_pair[core] = q_split[core]

    pl.semaphore_wait(barrier, pairs)

    q_cross = pltpu.make_async_remote_copy(
        src_ref=q_split.at[1 - core], dst_ref=q_pair.at[core], send_sem=qx_send, recv_sem=qx_recv,
        device_id=sib, device_id_type=MESH)
    q_cross.start()
    k_cross, v_cross = [], []
    for h in range(group):
        k_cross.append(pltpu.make_async_remote_copy(
            src_ref=k_hbm.at[:, columns(1 - core, h)], dst_ref=k_buf.at[h, pl.ds(key_dev, key_dev)],
            send_sem=k_send.at[h], recv_sem=k_recv.at[h], device_id=sib, device_id_type=MESH))
        k_cross[-1].start()
    for h in range(group):
        v_cross.append(pltpu.make_async_remote_copy(
            src_ref=v_hbm.at[:, columns(1 - core, h)], dst_ref=v_buf.at[h, pl.ds(key_dev, key_dev)],
            send_sem=v_send.at[h], recv_sem=v_recv.at[h], device_id=sib, device_id_type=MESH))
        v_cross[-1].start()

    q_cross.wait_recv()
    q_all[0] = q_pair[...].reshape(2 * maps, 128).astype(jnp.bfloat16)
    for_peers(lambda i: pltpu.make_async_remote_copy(
        src_ref=q_all.at[0], dst_ref=q_all.at[pairs - i], send_sem=qa_send, recv_sem=qa_recv,
        device_id=peer(i), device_id_type=MESH).start())

    gain_copy.wait()
    for part in range(2):
        for h in range(group):
            line = gain_own[pl.ds((core * group + h) * 2 + part, 1), :]
            gain_rows[part, h : h + 1, :] = line
            gain_rows[part, group + h : group + h + 1, :] = line
    lam_copy.wait()
    map_of = lax.broadcasted_iota(jnp.int32, (maps, tall), 0)
    sign = jnp.ones((maps, tall), jnp.float32)
    for h in range(group):
        sign = jnp.where(map_of == 2 * h + 1, -lam_own[core * group + h], sign)

    row_of = lax.broadcasted_iota(jnp.int32, (2 * tall, keys), 0)
    col_of = lax.broadcasted_iota(jnp.int32, (2 * tall, keys), 1)
    query = 2 * pair + jnp.where(row_of < tall, row_of, row_of - tall)
    query = jnp.where(query >= tall, query - tall, query)
    place = jnp.where(
        col_of < key_dev,
        (2 * pair + core) * key_dev + col_of,
        (2 * pair + 1 - core) * key_dev + col_of - key_dev)
    bias[...] = jnp.where(place <= tall * key_dev - tall + query, 0.0, LOWEST)
    lane = lax.broadcasted_iota(jnp.int32, (tall, 128), 1)
    scaling = 1.0 / math.sqrt(128)

    for h in range(group):
        k_locals[h].wait()
        k_cross[h].wait_recv()
    all_of(q_all.at[pl.ds(1, pairs - 1)], qa_recv)
    q_wide[...] = q_all[...].reshape(pairs * 2 * maps, 128).astype(jnp.float32)

    stats = jnp.zeros((tall, 128), jnp.float32)
    expos = []
    blank = jnp.zeros((tall, 128), jnp.bfloat16)
    for h in range(group):
        first = q_wide[pl.ds(2 * h, tall, stride=maps), :].astype(jnp.bfloat16)
        second = q_wide[pl.ds(2 * h + 1, tall, stride=maps), :].astype(jnp.bfloat16)
        both = jnp.concatenate(
            [jnp.concatenate([first, blank], axis=1), jnp.concatenate([blank, second], axis=1)], axis=0)
        score = lax.dot_general(
            both, k_buf[h], (((1,), (1,)), ((), ())), preferred_element_type=jnp.float32)
        score = score * scaling + bias[...]
        top = jnp.max(score, axis=1, keepdims=True)
        expo = jnp.exp(score - top)
        total = jnp.sum(expo, axis=1, keepdims=True)
        for side in range(2):
            m = 2 * h + side
            at = slice(side * tall, (side + 1) * tall)
            stats = jnp.where(lane == m, top[at], jnp.where(lane == maps + m, total[at], stats))
        expos.append(expo.astype(jnp.bfloat16))
    stat_send[...] = stats
    for_peers(lambda i: pltpu.make_async_remote_copy(
        src_ref=stat_send.at[pl.ds(2 * i, 2)], dst_ref=stat_recv.at[pl.ds(2 * i, 2)],
        send_sem=st_send, recv_sem=st_recv, device_id=peer(i), device_id_type=MESH).start())
    stat_recv[0:2] = stat_send[0:2]

    for h in range(group):
        v_locals[h].wait()
        v_cross[h].wait_recv()
    for h in range(group):
        summed = jnp.dot(expos[h], v_buf[h], preferred_element_type=jnp.float32)
        for side in range(2):
            for part in range(2):
                part_wide[part, pl.ds(2 * h + side, tall, stride=maps), :] = summed[
                    side * tall : (side + 1) * tall, part * 128 : part * 128 + 128]
    for part in range(2):
        part_send[:, part] = part_wide[part].reshape(pairs, 2 * maps, 128).astype(jnp.bfloat16)
    for_peers(lambda i: pltpu.make_async_remote_copy(
        src_ref=part_send.at[i], dst_ref=part_recv.at[i], send_sem=pa_send, recv_sem=pa_recv,
        device_id=peer(i), device_id_type=MESH).start())
    part_recv[0] = part_send[0]

    all_of(stat_recv.at[pl.ds(2, tall - 2)], st_recv)
    turned = stat_recv[...].T
    tops, totals = turned[0:maps], turned[maps : 2 * maps]
    even = lax.rem(lax.broadcasted_iota(jnp.int32, (maps, tall), 1), 2) == 0

    def per_query(array, reduce, fill):
        zero = reduce(jnp.where(even, array, fill), axis=1, keepdims=True)
        one = reduce(jnp.where(even, fill, array), axis=1, keepdims=True)
        return jnp.where(even, zero, one)

    factor = jnp.exp(tops - per_query(tops, jnp.max, -3e38))
    factor = factor * sign / per_query(factor * totals, jnp.sum, 0.0)

    all_of(part_recv.at[pl.ds(1, pairs - 1)], pa_recv)
    sums = [[jnp.zeros((maps, 128), jnp.float32) for _ in range(2)] for _ in range(2)]
    for s in range(pairs):
        for part in range(2):
            block = part_recv[s, part].astype(jnp.float32)
            for j in range(2):
                weight = factor[:, 2 * s + j : 2 * s + j + 1]
                sums[part][j] = sums[part][j] + weight * block[j * maps : (j + 1) * maps]
    diffs = []
    for part in range(2):
        for j in range(2):
            sum_pad[part, j * maps : (j + 1) * maps] = sums[part][j]
        diffs.append(
            sum_pad[part, pl.ds(0, maps, stride=2), :] + sum_pad[part, pl.ds(1, maps, stride=2), :])
    square = jnp.sum(diffs[0] * diffs[0] + diffs[1] * diffs[1], axis=1, keepdims=True) * (1.0 / 256)
    scale = jnp.sqrt(square + 1e-05)
    for part in range(2):
        normed = diffs[part] / scale * gain_rows[part]
        for j in range(2):
            fin_send[j, part * group : (part + 1) * group, :] = normed[j * group : (j + 1) * group]
    fin_cross = pltpu.make_async_remote_copy(
        src_ref=fin_send.at[1 - core], dst_ref=fin_recv, send_sem=fx_send, recv_sem=fx_recv,
        device_id=sib, device_id_type=MESH)
    fin_cross.start()

    def put(which, lines):
        for part in range(2):
            for h in range(group):
                at = pl.ds(pl.multiple_of(which * width + h * 256 + part * 128, 128), 128)
                out_ref[:, at] = lines[part * group + h : part * group + h + 1]

    put(core, fin_send[core])
    q_cross.wait_send()
    for h in range(group):
        k_cross[h].wait_send()
        v_cross[h].wait_send()
    all_of(q_all.at[pl.ds(1, pairs - 1)], qa_send)
    all_of(stat_send.at[pl.ds(2, tall - 2)], st_send)
    all_of(part_send.at[pl.ds(1, pairs - 1)], pa_send)
    fin_cross.wait()
    put(1 - core, fin_recv[...])


def shards(queries, key_maps, values, lambdas, norm_gain):
    rows, cols = lax.axis_size("qrow"), lax.axis_size("kcol")
    heads = lambdas.shape[0]
    key_dev = key_maps.shape[0]
    assert queries.shape[0] == 1 and heads == 8
    assert key_maps.shape[1] == 2048 and values.shape[1] == 2048
    assert cols % 2 == 0 and rows * cols <= 2 * key_dev
    group = heads // 2
    maps = 2 * group
    pairs = rows * cols // 2
    tall = 2 * pairs
    f32, bf16 = jnp.float32, jnp.bfloat16
    dma = pltpu.SemaphoreType.DMA
    in_hbm = pl.BlockSpec(memory_space=pltpu.HBM)
    out = pl.pallas_call(
        functools.partial(kernel, rows, cols, key_dev, heads),
        out_shape=jax.ShapeDtypeStruct((1, 2048), f32),
        in_specs=[in_hbm] * 5,
        out_specs=pl.BlockSpec(memory_space=pltpu.VMEM),
        scratch_shapes=[
            pltpu.VMEM((1, 2048), bf16),
            pltpu.SMEM((heads,), f32),
            pltpu.VMEM((16, 128), f32),
            pltpu.VMEM((group, 2 * key_dev, 256), bf16),
            pltpu.VMEM((group, 2 * key_dev, 256), bf16),
            pltpu.VMEM((2, maps, 128), f32),
            pltpu.VMEM((2, maps, 128), f32),
            pltpu.VMEM((pairs, 2 * maps, 128), bf16),
            pltpu.VMEM((pairs * 2 * maps, 128), f32),
            pltpu.VMEM((2 * tall, 2 * key_dev), f32),
            pltpu.VMEM((tall, 128), f32),
            pltpu.VMEM((tall, 128), f32),
            pltpu.VMEM((2, pairs * 2 * maps, 128), f32),
            pltpu.VMEM((pairs, 2, 2 * maps, 128), bf16),
            pltpu.VMEM((pairs, 2, 2 * maps, 128), bf16),
            pltpu.VMEM((2, 2 * maps, 128), f32),
            pltpu.VMEM((2, 2 * group, 128), f32),
            pltpu.VMEM((2, 2 * group, 128), f32),
            pltpu.VMEM((2 * group, 128), f32),
            dma, dma, dma,
            dma((group,)), dma((group,)), dma((group,)), dma((group,)), dma((group,)), dma((group,)),
            dma, dma, dma, dma, dma, dma, dma, dma, dma, dma,
        ],
        compiler_params=pltpu.CompilerParams(
            collective_id=0, has_side_effects=True, vmem_limit_bytes=40 * 2**20),
        cost_estimate=pl.CostEstimate(
            flops=6 * tall * 2 * key_dev * 1024, bytes_accessed=4 * key_dev * 2048, transcendentals=0),
    )(queries, key_maps, values, lambdas, norm_gain.reshape(16, 128))
    return out.astype(bf16)


def solution(mesh):
    in_specs = (
        P(("qrow", "kcol"), None),
        P(("qrow", "kcol"), None),
        P(("qrow", "kcol"), None),
        P(),
        P(),
    )
    out_specs = P(("qrow", "kcol"), None)
    return jax.shard_map(shards, mesh=mesh, in_specs=in_specs, out_specs=out_specs, check_vma=False)
```

```python
import functools
import math

import jax
import jax.numpy as jnp
from jax import lax
from jax.experimental import pallas as pl
from jax.experimental.pallas import tpu as pltpu
from jax.sharding import PartitionSpec as P

MESH = pl.DeviceIdType.MESH
LOWEST = -1e30


def kernel(
    rows, cols, key_dev, heads,
    q_hbm, k_hbm, v_hbm, lam_hbm, gain_hbm,
    out_ref,
    q_own, lam_own, gain_own, k_buf, v_buf, q_split, q_pair, q_all, q_wide, bias,
    stat_send, stat_recv, part_wide, part_send, part_recv, sum_pad, gain_rows, fin_send, fin_recv,
    q_sem, lam_sem, gain_sem, k_own_sem, v_own_sem, k_send, k_recv, v_send, v_recv,
    qx_send, qx_recv, qa_send, qa_recv, st_send, st_recv, pa_send, pa_recv, fx_send, fx_recv,
):
    row = lax.axis_index("qrow")
    col = lax.axis_index("kcol")
    core = lax.rem(col, 2)
    half_cols = cols // 2
    pairs = rows * half_cols
    pair = row * half_cols + lax.div(col, 2)
    sib = (row, col + 1 - 2 * core)
    group = heads // 2
    maps = 2 * group
    width = group * 256
    tall = 2 * pairs
    keys = 2 * key_dev

    def peer(offset):
        other = pair + offset
        other = jnp.where(other >= pairs, other - pairs, other)
        its_row = lax.div(other, half_cols)
        return (its_row, 2 * (other - its_row * half_cols) + core)

    def for_peers(step):
        if pairs <= 16:
            for i in range(1, pairs):
                step(i)
        else:
            lax.fori_loop(1, pairs, lambda i, carry: (step(i), carry)[1], 0)

    def columns(which, h):
        return pl.ds(pl.multiple_of(which * width + h * 256, 128), 256)

    def all_of(ref, sem):
        pltpu.make_async_copy(ref, ref, sem).wait()

    q_copy = pltpu.make_async_copy(q_hbm, q_own, q_sem)
    q_copy.start()
    barrier = pltpu.get_barrier_semaphore()
    for_peers(lambda i: pl.semaphore_signal(barrier, inc=1, device_id=peer(i), device_id_type=MESH))
    pl.semaphore_signal(barrier, inc=1, device_id=sib, device_id_type=MESH)

    lam_copy = pltpu.make_async_copy(lam_hbm, lam_own, lam_sem)
    lam_copy.start()
    gain_copy = pltpu.make_async_copy(gain_hbm, gain_own, gain_sem)
    gain_copy.start()
    k_locals, v_locals = [], []
    for h in range(group):
        k_locals.append(pltpu.make_async_copy(
            k_hbm.at[:, columns(core, h)], k_buf.at[h, pl.ds(0, key_dev)], k_own_sem.at[h]))
        k_locals[-1].start()
    for h in range(group):
        v_locals.append(pltpu.make_async_copy(
            v_hbm.at[:, columns(core, h)], v_buf.at[h, pl.ds(0, key_dev)], v_own_sem.at[h]))
        v_locals[-1].start()

    q_copy.wait()
    for g in range(2):
        for m in range(maps):
            at = (g * maps + m) * 128
            q_split[g, m : m + 1, :] = q_own[:, at : at + 128].astype(jnp.float32)
    q_pair[core] = q_split[core]

    pl.semaphore_wait(barrier, pairs)

    q_cross = pltpu.make_async_remote_copy(
        src_ref=q_split.at[1 - core], dst_ref=q_pair.at[core], send_sem=qx_send, recv_sem=qx_recv,
        device_id=sib, device_id_type=MESH)
    q_cross.start()
    k_cross, v_cross = [], []
    for h in range(group):
        k_cross.append(pltpu.make_async_remote_copy(
            src_ref=k_hbm.at[:, columns(1 - core, h)], dst_ref=k_buf.at[h, pl.ds(key_dev, key_dev)],
            send_sem=k_send.at[h], recv_sem=k_recv.at[h], device_id=sib, device_id_type=MESH))
        k_cross[-1].start()

    q_cross.wait_recv()
    q_all[0] = q_pair[...].reshape(2 * maps, 128).astype(jnp.bfloat16)
    for_peers(lambda i: pltpu.make_async_remote_copy(
        src_ref=q_all.at[0], dst_ref=q_all.at[pairs - i], send_sem=qa_send, recv_sem=qa_recv,
        device_id=peer(i), device_id_type=MESH).start())
    for h in range(group):
        v_cross.append(pltpu.make_async_remote_copy(
            src_ref=v_hbm.at[:, columns(1 - core, h)], dst_ref=v_buf.at[h, pl.ds(key_dev, key_dev)],
            send_sem=v_send.at[h], recv_sem=v_recv.at[h], device_id=sib, device_id_type=MESH))
        v_cross[-1].start()

    gain_copy.wait()
    for part in range(2):
        for h in range(group):
            line = gain_own[pl.ds((core * group + h) * 2 + part, 1), :]
            gain_rows[part, h : h + 1, :] = line
            gain_rows[part, group + h : group + h + 1, :] = line
    lam_copy.wait()
    map_of = lax.broadcasted_iota(jnp.int32, (maps, tall), 0)
    sign = jnp.ones((maps, tall), jnp.float32)
    for h in range(group):
        sign = jnp.where(map_of == 2 * h + 1, -lam_own[core * group + h], sign)

    row_of = lax.broadcasted_iota(jnp.int32, (2 * tall, keys), 0)
    col_of = lax.broadcasted_iota(jnp.int32, (2 * tall, keys), 1)
    query = 2 * pair + jnp.where(row_of < tall, row_of, row_of - tall)
    query = jnp.where(query >= tall, query - tall, query)
    place = jnp.where(
        col_of < key_dev,
        (2 * pair + core) * key_dev + col_of,
        (2 * pair + 1 - core) * key_dev + col_of - key_dev)
    bias[...] = jnp.where(place <= tall * key_dev - tall + query, 0.0, LOWEST)
    lane = lax.broadcasted_iota(jnp.int32, (tall, 128), 1)
    scaling = 1.0 / math.sqrt(128)

    for h in range(group):
        k_locals[h].wait()
        k_cross[h].wait_recv()
    all_of(q_all.at[pl.ds(1, pairs - 1)], qa_recv)
    q_wide[...] = q_all[...].reshape(pairs * 2 * maps, 128).astype(jnp.float32)

    stats = jnp.zeros((tall, 128), jnp.float32)
    expos = []
    blank = jnp.zeros((tall, 128), jnp.bfloat16)
    for h in range(group):
        first = q_wide[pl.ds(2 * h, tall, stride=maps), :].astype(jnp.bfloat16)
        second = q_wide[pl.ds(2 * h + 1, tall, stride=maps), :].astype(jnp.bfloat16)
        both = jnp.concatenate(
            [jnp.concatenate([first, blank], axis=1), jnp.concatenate([blank, second], axis=1)], axis=0)
        score = lax.dot_general(
            both, k_buf[h], (((1,), (1,)), ((), ())), preferred_element_type=jnp.float32)
        score = score * scaling + bias[...]
        top = jnp.max(score, axis=1, keepdims=True)
        expo = jnp.exp(score - top)
        total = jnp.sum(expo, axis=1, keepdims=True)
        for side in range(2):
            m = 2 * h + side
            at = slice(side * tall, (side + 1) * tall)
            stats = jnp.where(lane == m, top[at], jnp.where(lane == maps + m, total[at], stats))
        expos.append(expo.astype(jnp.bfloat16))
    stat_send[...] = stats
    for_peers(lambda i: pltpu.make_async_remote_copy(
        src_ref=stat_send.at[pl.ds(2 * i, 2)], dst_ref=stat_recv.at[pl.ds(2 * i, 2)],
        send_sem=st_send, recv_sem=st_recv, device_id=peer(i), device_id_type=MESH).start())
    stat_recv[0:2] = stat_send[0:2]

    for h in range(group):
        v_locals[h].wait()
        v_cross[h].wait_recv()
    for h in range(group):
        summed = jnp.dot(expos[h], v_buf[h], preferred_element_type=jnp.float32)
        for side in range(2):
            for part in range(2):
                part_wide[part, pl.ds(2 * h + side, tall, stride=maps), :] = summed[
                    side * tall : (side + 1) * tall, part * 128 : part * 128 + 128]
    for part in range(2):
        part_send[:, part] = part_wide[part].reshape(pairs, 2 * maps, 128).astype(jnp.bfloat16)
    for_peers(lambda i: pltpu.make_async_remote_copy(
        src_ref=part_send.at[i], dst_ref=part_recv.at[i], send_sem=pa_send, recv_sem=pa_recv,
        device_id=peer(i), device_id_type=MESH).start())
    part_recv[0] = part_send[0]

    all_of(stat_recv.at[pl.ds(2, tall - 2)], st_recv)
    turned = stat_recv[...].T
    tops, totals = turned[0:maps], turned[maps : 2 * maps]
    even = lax.rem(lax.broadcasted_iota(jnp.int32, (maps, tall), 1), 2) == 0

    def per_query(array, reduce, fill):
        zero = reduce(jnp.where(even, array, fill), axis=1, keepdims=True)
        one = reduce(jnp.where(even, fill, array), axis=1, keepdims=True)
        return jnp.where(even, zero, one)

    factor = jnp.exp(tops - per_query(tops, jnp.max, -3e38))
    factor = factor * sign / per_query(factor * totals, jnp.sum, 0.0)

    all_of(part_recv.at[pl.ds(1, pairs - 1)], pa_recv)
    sums = [[jnp.zeros((maps, 128), jnp.float32) for _ in range(2)] for _ in range(2)]
    for s in range(pairs):
        for part in range(2):
            block = part_recv[s, part].astype(jnp.float32)
            for j in range(2):
                weight = factor[:, 2 * s + j : 2 * s + j + 1]
                sums[part][j] = sums[part][j] + weight * block[j * maps : (j + 1) * maps]
    diffs = []
    for part in range(2):
        for j in range(2):
            sum_pad[part, j * maps : (j + 1) * maps] = sums[part][j]
        diffs.append(
            sum_pad[part, pl.ds(0, maps, stride=2), :] + sum_pad[part, pl.ds(1, maps, stride=2), :])
    square = jnp.sum(diffs[0] * diffs[0] + diffs[1] * diffs[1], axis=1, keepdims=True) * (1.0 / 256)
    scale = jnp.sqrt(square + 1e-05)
    for part in range(2):
        normed = diffs[part] / scale * gain_rows[part]
        for j in range(2):
            fin_send[j, part * group : (part + 1) * group, :] = normed[j * group : (j + 1) * group]
    fin_cross = pltpu.make_async_remote_copy(
        src_ref=fin_send.at[1 - core], dst_ref=fin_recv, send_sem=fx_send, recv_sem=fx_recv,
        device_id=sib, device_id_type=MESH)
    fin_cross.start()

    def put(which, lines):
        for part in range(2):
            for h in range(group):
                at = pl.ds(pl.multiple_of(which * width + h * 256 + part * 128, 128), 128)
                out_ref[:, at] = lines[part * group + h : part * group + h + 1]

    put(core, fin_send[core])
    q_cross.wait_send()
    for h in range(group):
        k_cross[h].wait_send()
        v_cross[h].wait_send()
    all_of(q_all.at[pl.ds(1, pairs - 1)], qa_send)
    all_of(stat_send.at[pl.ds(2, tall - 2)], st_send)
    all_of(part_send.at[pl.ds(1, pairs - 1)], pa_send)
    fin_cross.wait()
    put(1 - core, fin_recv[...])


def shards(queries, key_maps, values, lambdas, norm_gain):
    rows, cols = lax.axis_size("qrow"), lax.axis_size("kcol")
    heads = lambdas.shape[0]
    key_dev = key_maps.shape[0]
    assert queries.shape[0] == 1 and heads == 8
    assert key_maps.shape[1] == 2048 and values.shape[1] == 2048
    assert cols % 2 == 0 and rows * cols <= 2 * key_dev
    group = heads // 2
    maps = 2 * group
    pairs = rows * cols // 2
    tall = 2 * pairs
    f32, bf16 = jnp.float32, jnp.bfloat16
    dma = pltpu.SemaphoreType.DMA
    in_hbm = pl.BlockSpec(memory_space=pltpu.HBM)
    out = pl.pallas_call(
        functools.partial(kernel, rows, cols, key_dev, heads),
        out_shape=jax.ShapeDtypeStruct((1, 2048), f32),
        in_specs=[in_hbm] * 5,
        out_specs=pl.BlockSpec(memory_space=pltpu.VMEM),
        scratch_shapes=[
            pltpu.VMEM((1, 2048), bf16),
            pltpu.SMEM((heads,), f32),
            pltpu.VMEM((16, 128), f32),
            pltpu.VMEM((group, 2 * key_dev, 256), bf16),
            pltpu.VMEM((group, 2 * key_dev, 256), bf16),
            pltpu.VMEM((2, maps, 128), f32),
            pltpu.VMEM((2, maps, 128), f32),
            pltpu.VMEM((pairs, 2 * maps, 128), bf16),
            pltpu.VMEM((pairs * 2 * maps, 128), f32),
            pltpu.VMEM((2 * tall, 2 * key_dev), f32),
            pltpu.VMEM((tall, 128), f32),
            pltpu.VMEM((tall, 128), f32),
            pltpu.VMEM((2, pairs * 2 * maps, 128), f32),
            pltpu.VMEM((pairs, 2, 2 * maps, 128), bf16),
            pltpu.VMEM((pairs, 2, 2 * maps, 128), bf16),
            pltpu.VMEM((2, 2 * maps, 128), f32),
            pltpu.VMEM((2, 2 * group, 128), f32),
            pltpu.VMEM((2, 2 * group, 128), f32),
            pltpu.VMEM((2 * group, 128), f32),
            dma, dma, dma,
            dma((group,)), dma((group,)), dma((group,)), dma((group,)), dma((group,)), dma((group,)),
            dma, dma, dma, dma, dma, dma, dma, dma, dma, dma,
        ],
        compiler_params=pltpu.CompilerParams(
            collective_id=0, has_side_effects=True),
        cost_estimate=pl.CostEstimate(
            flops=6 * tall * 2 * key_dev * 1024, bytes_accessed=4 * key_dev * 2048, transcendentals=0),
    )(queries, key_maps, values, lambdas, norm_gain.reshape(16, 128))
    return out.astype(bf16)


def solution(mesh):
    in_specs = (
        P(("qrow", "kcol"), None),
        P(("qrow", "kcol"), None),
        P(("qrow", "kcol"), None),
        P(),
        P(),
    )
    out_specs = P(("qrow", "kcol"), None)
    return jax.shard_map(shards, mesh=mesh, in_specs=in_specs, out_specs=out_specs, check_vma=False)
```

```python
import functools
import math

import jax
import jax.numpy as jnp
from jax import lax
from jax.experimental import pallas as pl
from jax.experimental.pallas import tpu as pltpu
from jax.sharding import PartitionSpec as P

MESH = pl.DeviceIdType.MESH
LOWEST = -1e30


def kernel(
    rows, cols, key_dev, heads,
    q_hbm, k_hbm, v_hbm, lam_hbm, gain_hbm,
    out_ref,
    q_own, lam_own, gain_own, k_buf, v_buf, q_split, q_pair, q_all, q_wide, bias,
    stat_send, stat_recv, part_wide, part_send, part_recv, sum_pad,
    q_sem, lam_sem, gain_sem, k_own_sem, v_own_sem, k_send, k_recv, v_send, v_recv,
    qx_send, qx_recv, qa_send, qa_recv, st_send, st_recv, pa_send, pa_recv,
):
    row = lax.axis_index("qrow")
    col = lax.axis_index("kcol")
    core = lax.rem(col, 2)
    half_cols = cols // 2
    pairs = rows * half_cols
    pair = row * half_cols + lax.div(col, 2)
    sib = (row, col + 1 - 2 * core)
    group = heads // 2
    maps = 2 * group
    width = group * 256
    tall = 2 * pairs
    keys = 2 * key_dev

    def peer(offset, its_core):
        other = pair + offset
        other = jnp.where(other >= pairs, other - pairs, other)
        its_row = lax.div(other, half_cols)
        return (its_row, 2 * (other - its_row * half_cols) + its_core)

    def for_peers(step):
        if pairs <= 16:
            for i in range(1, pairs):
                step(i)
        else:
            lax.fori_loop(1, pairs, lambda i, carry: (step(i), carry)[1], 0)

    def columns(which, h):
        return pl.ds(pl.multiple_of(which * width + h * 256, 128), 256)

    def all_of(ref, sem):
        pltpu.make_async_copy(ref, ref, sem).wait()

    q_copy = pltpu.make_async_copy(q_hbm, q_own, q_sem)
    q_copy.start()
    barrier = pltpu.get_barrier_semaphore()

    def greet(i):
        for j in range(2):
            pl.semaphore_signal(barrier, inc=1, device_id=peer(i, j), device_id_type=MESH)

    pl.semaphore_signal(barrier, inc=1, device_id=sib, device_id_type=MESH)
    for_peers(greet)

    lam_copy = pltpu.make_async_copy(lam_hbm, lam_own, lam_sem)
    lam_copy.start()
    gain_copy = pltpu.make_async_copy(gain_hbm, gain_own, gain_sem)
    gain_copy.start()
    k_locals, v_locals = [], []
    for h in range(group):
        k_locals.append(pltpu.make_async_copy(
            k_hbm.at[:, columns(core, h)], k_buf.at[h, pl.ds(0, key_dev)], k_own_sem.at[h]))
        k_locals[-1].start()
    for h in range(group):
        v_locals.append(pltpu.make_async_copy(
            v_hbm.at[:, columns(core, h)], v_buf.at[h, pl.ds(0, key_dev)], v_own_sem.at[h]))
        v_locals[-1].start()

    q_copy.wait()
    for g in range(2):
        for m in range(maps):
            at = (g * maps + m) * 128
            q_split[g, m : m + 1, :] = q_own[:, at : at + 128].astype(jnp.float32)
    q_pair[core] = q_split[core]

    pl.semaphore_wait(barrier, tall - 1)

    q_cross = pltpu.make_async_remote_copy(
        src_ref=q_split.at[1 - core], dst_ref=q_pair.at[core], send_sem=qx_send, recv_sem=qx_recv,
        device_id=sib, device_id_type=MESH)
    q_cross.start()
    k_cross, v_cross = [], []
    for h in range(group):
        k_cross.append(pltpu.make_async_remote_copy(
            src_ref=k_hbm.at[:, columns(1 - core, h)], dst_ref=k_buf.at[h, pl.ds(key_dev, key_dev)],
            send_sem=k_send.at[h], recv_sem=k_recv.at[h], device_id=sib, device_id_type=MESH))
        k_cross[-1].start()

    q_cross.wait_recv()
    q_all[0] = q_pair[...].reshape(2 * maps, 128).astype(jnp.bfloat16)
    for_peers(lambda i: pltpu.make_async_remote_copy(
        src_ref=q_all.at[0], dst_ref=q_all.at[pairs - i], send_sem=qa_send, recv_sem=qa_recv,
        device_id=peer(i, core), device_id_type=MESH).start())
    for h in range(group):
        v_cross.append(pltpu.make_async_remote_copy(
            src_ref=v_hbm.at[:, columns(1 - core, h)], dst_ref=v_buf.at[h, pl.ds(key_dev, key_dev)],
            send_sem=v_send.at[h], recv_sem=v_recv.at[h], device_id=sib, device_id_type=MESH))
        v_cross[-1].start()

    lam_copy.wait()
    map_of = lax.broadcasted_iota(jnp.int32, (maps, tall), 0)
    low = lax.broadcasted_iota(jnp.int32, (maps, tall), 1) < pairs
    sign = jnp.ones((maps, tall), jnp.float32)
    for h in range(group):
        sign = jnp.where(map_of == 2 * h + 1, jnp.where(low, -lam_own[h], -lam_own[group + h]), sign)

    row_of = lax.broadcasted_iota(jnp.int32, (2 * tall, keys), 0)
    col_of = lax.broadcasted_iota(jnp.int32, (2 * tall, keys), 1)
    query = 2 * pair + jnp.where(row_of < tall, row_of, row_of - tall)
    query = jnp.where(query >= tall, query - tall, query)
    place = jnp.where(
        col_of < key_dev,
        (2 * pair + core) * key_dev + col_of,
        (2 * pair + 1 - core) * key_dev + col_of - key_dev)
    bias[...] = jnp.where(place <= tall * key_dev - tall + query, 0.0, LOWEST)
    lane = lax.broadcasted_iota(jnp.int32, (tall, 128), 1)
    scaling = 1.0 / math.sqrt(128)

    for h in range(group):
        k_locals[h].wait()
        k_cross[h].wait_recv()
    all_of(q_all.at[pl.ds(1, pairs - 1)], qa_recv)
    q_wide[...] = q_all[...].reshape(pairs * 2 * maps, 128).astype(jnp.float32)

    stats = jnp.zeros((tall, 128), jnp.float32)
    expos = []
    blank = jnp.zeros((tall, 128), jnp.bfloat16)
    for h in range(group):
        first = q_wide[pl.ds(2 * h, tall, stride=maps), :].astype(jnp.bfloat16)
        second = q_wide[pl.ds(2 * h + 1, tall, stride=maps), :].astype(jnp.bfloat16)
        both = jnp.concatenate(
            [jnp.concatenate([first, blank], axis=1), jnp.concatenate([blank, second], axis=1)], axis=0)
        score = lax.dot_general(
            both, k_buf[h], (((1,), (1,)), ((), ())), preferred_element_type=jnp.float32)
        score = score * scaling + bias[...]
        top = jnp.max(score, axis=1, keepdims=True)
        expo = jnp.exp(score - top)
        total = jnp.sum(expo, axis=1, keepdims=True)
        for side in range(2):
            m = 2 * h + side
            at = slice(side * tall, (side + 1) * tall)
            stats = jnp.where(lane == m, top[at], jnp.where(lane == maps + m, total[at], stats))
        expos.append(expo.astype(jnp.bfloat16))
    stat_send[...] = stats

    def send_stats(t, where):
        pltpu.make_async_remote_copy(
            src_ref=stat_send.at[pl.ds(t, 1)], dst_ref=stat_recv.at[pl.ds(core * pairs + t // 2, 1)],
            send_sem=st_send, recv_sem=st_recv, device_id=where, device_id_type=MESH).start()

    def send_part(t, where):
        pltpu.make_async_remote_copy(
            src_ref=part_send.at[t], dst_ref=part_recv.at[t // 2 * 2 + core],
            send_sem=pa_send, recv_sem=pa_recv, device_id=where, device_id_type=MESH).start()

    def to_all(send):
        for_peers(lambda i: [send(2 * i + j, peer(i, j)) for j in range(2)])
        send(1 - core, sib)

    to_all(send_stats)
    stat_recv[pl.ds(core * pairs, 1)] = stat_send[pl.ds(core, 1)]

    for h in range(group):
        v_locals[h].wait()
        v_cross[h].wait_recv()
    for h in range(group):
        summed = jnp.dot(expos[h], v_buf[h], preferred_element_type=jnp.float32)
        for side in range(2):
            for part in range(2):
                part_wide[pl.ds(part * maps + 2 * h + side, tall, stride=2 * maps), :] = summed[
                    side * tall : (side + 1) * tall, part * 128 : part * 128 + 128]
    part_send[...] = part_wide[...].reshape(tall, 2 * maps, 128).astype(jnp.bfloat16)
    to_all(send_part)
    part_recv[core] = part_send[core]

    all_of(stat_recv.at[pl.ds(1, tall - 1)], st_recv)
    turned = stat_recv[...].T
    tops, totals = turned[0:maps], turned[maps : 2 * maps]

    def per_group(array, reduce, fill):
        zero = reduce(jnp.where(low, array, fill), axis=1, keepdims=True)
        one = reduce(jnp.where(low, fill, array), axis=1, keepdims=True)
        return jnp.where(low, zero, one)

    factor = jnp.exp(tops - per_group(tops, jnp.max, -3e38))
    factor = factor * sign / per_group(factor * totals, jnp.sum, 0.0)
    gain_copy.wait()

    all_of(part_recv.at[pl.ds(1, tall - 1)], pa_recv)
    sums = [[jnp.zeros((maps, 128), jnp.float32) for _ in range(2)] for _ in range(2)]
    for s in range(pairs):
        for g in range(2):
            weight = factor[:, g * pairs + s : g * pairs + s + 1]
            block = part_recv[2 * s + g].astype(jnp.float32)
            for part in range(2):
                sums[part][g] = sums[part][g] + weight * block[part * maps : (part + 1) * maps]
    diffs = []
    for part in range(2):
        for g in range(2):
            sum_pad[part, g * maps : (g + 1) * maps] = sums[part][g]
        diffs.append(
            sum_pad[part, pl.ds(0, heads, stride=2), :] + sum_pad[part, pl.ds(1, heads, stride=2), :])
    square = jnp.sum(diffs[0] * diffs[0] + diffs[1] * diffs[1], axis=1, keepdims=True) * (1.0 / 256)
    scale = jnp.sqrt(square + 1e-05)
    normed = [diffs[part] / scale * gain_own[pl.ds(part, heads, stride=2), :] for part in range(2)]
    line = jnp.concatenate([normed[part][h : h + 1] for h in range(heads) for part in range(2)], axis=1)
    out_ref[...] = line.astype(jnp.bfloat16)

    q_cross.wait_send()
    for h in range(group):
        k_cross[h].wait_send()
        v_cross[h].wait_send()
    all_of(q_all.at[pl.ds(1, pairs - 1)], qa_send)
    all_of(stat_send.at[pl.ds(1, tall - 1)], st_send)
    all_of(part_send.at[pl.ds(1, tall - 1)], pa_send)


def shards(queries, key_maps, values, lambdas, norm_gain):
    rows, cols = lax.axis_size("qrow"), lax.axis_size("kcol")
    heads = lambdas.shape[0]
    key_dev = key_maps.shape[0]
    assert queries.shape[0] == 1 and heads == 8
    assert key_maps.shape[1] == 2048 and values.shape[1] == 2048
    assert cols % 2 == 0 and rows * cols <= 2 * key_dev
    group = heads // 2
    maps = 2 * group
    pairs = rows * cols // 2
    tall = 2 * pairs
    f32, bf16 = jnp.float32, jnp.bfloat16
    dma = pltpu.SemaphoreType.DMA
    in_hbm = pl.BlockSpec(memory_space=pltpu.HBM)
    out = pl.pallas_call(
        functools.partial(kernel, rows, cols, key_dev, heads),
        out_shape=jax.ShapeDtypeStruct((1, 2048), bf16),
        in_specs=[in_hbm] * 5,
        out_specs=pl.BlockSpec(memory_space=pltpu.VMEM),
        scratch_shapes=[
            pltpu.VMEM((1, 2048), bf16),
            pltpu.SMEM((heads,), f32),
            pltpu.VMEM((16, 128), f32),
            pltpu.VMEM((group, 2 * key_dev, 256), bf16),
            pltpu.VMEM((group, 2 * key_dev, 256), bf16),
            pltpu.VMEM((2, maps, 128), f32),
            pltpu.VMEM((2, maps, 128), f32),
            pltpu.VMEM((pairs, 2 * maps, 128), bf16),
            pltpu.VMEM((pairs * 2 * maps, 128), f32),
            pltpu.VMEM((2 * tall, 2 * key_dev), f32),
            pltpu.VMEM((tall, 128), f32),
            pltpu.VMEM((tall, 128), f32),
            pltpu.VMEM((tall * 2 * maps, 128), f32),
            pltpu.VMEM((tall, 2 * maps, 128), bf16),
            pltpu.VMEM((tall, 2 * maps, 128), bf16),
            pltpu.VMEM((2, 2 * maps, 128), f32),
            dma, dma, dma,
            dma((group,)), dma((group,)), dma((group,)), dma((group,)), dma((group,)), dma((group,)),
            dma, dma, dma, dma, dma, dma, dma, dma,
        ],
        compiler_params=pltpu.CompilerParams(
            collective_id=0, has_side_effects=True),
        cost_estimate=pl.CostEstimate(
            flops=6 * tall * 2 * key_dev * 1024, bytes_accessed=4 * key_dev * 2048, transcendentals=0),
    )(queries, key_maps, values, lambdas, norm_gain.reshape(16, 128))
    return out


def solution(mesh):
    in_specs = (
        P(("qrow", "kcol"), None),
        P(("qrow", "kcol"), None),
        P(("qrow", "kcol"), None),
        P(),
        P(),
    )
    out_specs = P(("qrow", "kcol"), None)
    return jax.shard_map(shards, mesh=mesh, in_specs=in_specs, out_specs=out_specs, check_vma=False)
```

```python
import functools
import math

import jax
import jax.numpy as jnp
from jax import lax
from jax.experimental import pallas as pl
from jax.experimental.pallas import tpu as pltpu
from jax.sharding import PartitionSpec as P

MESH = pl.DeviceIdType.MESH
LOWEST = -1e30


def kernel(
    rows, cols, key_dev, heads,
    q_hbm, k_hbm, v_hbm, lam_hbm, gain_hbm,
    out_ref,
    q_own, lam_own, gain_own, k_buf, v_buf, q_split, q_wide, bias,
    stat_send, stat_recv, part_wide, part_send, part_recv, sum_pad,
    q_sem, lam_sem, gain_sem, k_own_sem, v_own_sem, k_send, k_recv, v_send, v_recv,
    qa_send, qa_recv, st_send, st_recv, pa_send, pa_recv,
):
    row = lax.axis_index("qrow")
    col = lax.axis_index("kcol")
    core = lax.rem(col, 2)
    half_cols = cols // 2
    pairs = rows * half_cols
    pair = row * half_cols + lax.div(col, 2)
    sib = (row, col + 1 - 2 * core)
    group = heads // 2
    maps = 2 * group
    width = group * 256
    tall = 2 * pairs
    keys = 2 * key_dev

    def peer(offset, its_core):
        other = pair + offset
        other = jnp.where(other >= pairs, other - pairs, other)
        its_row = lax.div(other, half_cols)
        return (its_row, 2 * (other - its_row * half_cols) + its_core)

    def for_peers(step):
        if pairs <= 16:
            for i in range(1, pairs):
                step(i)
        else:
            lax.fori_loop(1, pairs, lambda i, carry: (step(i), carry)[1], 0)

    def columns(which, h):
        return pl.ds(pl.multiple_of(which * width + h * 256, 128), 256)

    def all_of(ref, sem):
        pltpu.make_async_copy(ref, ref, sem).wait()

    q_copy = pltpu.make_async_copy(q_hbm, q_own, q_sem)
    q_copy.start()
    barrier = pltpu.get_barrier_semaphore()

    def greet(i):
        for j in range(2):
            pl.semaphore_signal(barrier, inc=1, device_id=peer(i, j), device_id_type=MESH)

    pl.semaphore_signal(barrier, inc=1, device_id=sib, device_id_type=MESH)
    for_peers(greet)

    lam_copy = pltpu.make_async_copy(lam_hbm, lam_own, lam_sem)
    lam_copy.start()
    gain_copy = pltpu.make_async_copy(gain_hbm, gain_own, gain_sem)
    gain_copy.start()
    k_locals, v_locals = [], []
    for h in range(group):
        k_locals.append(pltpu.make_async_copy(
            k_hbm.at[:, columns(core, h)], k_buf.at[h, pl.ds(0, key_dev)], k_own_sem.at[h]))
        k_locals[-1].start()
    for h in range(group):
        v_locals.append(pltpu.make_async_copy(
            v_hbm.at[:, columns(core, h)], v_buf.at[h, pl.ds(0, key_dev)], v_own_sem.at[h]))
        v_locals[-1].start()

    q_copy.wait()
    for g in range(2):
        for m in range(maps):
            at = (g * maps + m) * 128
            q_split[g, m : m + 1, :] = q_own[:, at : at + 128].astype(jnp.float32)

    def to_all(send):
        for_peers(lambda i: [send(2 * i + j, peer(i, j), j) for j in range(2)])
        send(1 - core, sib, 1 - core)

    def send_query(t, where, its_core):
        back = lax.rem(tall - (t - its_core), tall) + core
        pltpu.make_async_remote_copy(
            src_ref=q_split.at[its_core], dst_ref=q_wide.at[pl.ds(pl.multiple_of(back * maps, 8), maps)],
            send_sem=qa_send, recv_sem=qa_recv, device_id=where, device_id_type=MESH).start()

    pl.semaphore_wait(barrier, tall - 1)

    to_all(send_query)
    q_wide[pl.ds(pl.multiple_of(core * maps, 8), maps)] = q_split[core]
    k_cross, v_cross = [], []
    for h in range(group):
        k_cross.append(pltpu.make_async_remote_copy(
            src_ref=k_hbm.at[:, columns(1 - core, h)], dst_ref=k_buf.at[h, pl.ds(key_dev, key_dev)],
            send_sem=k_send.at[h], recv_sem=k_recv.at[h], device_id=sib, device_id_type=MESH))
        k_cross[-1].start()

    for h in range(group):
        v_cross.append(pltpu.make_async_remote_copy(
            src_ref=v_hbm.at[:, columns(1 - core, h)], dst_ref=v_buf.at[h, pl.ds(key_dev, key_dev)],
            send_sem=v_send.at[h], recv_sem=v_recv.at[h], device_id=sib, device_id_type=MESH))
        v_cross[-1].start()

    lam_copy.wait()
    map_of = lax.broadcasted_iota(jnp.int32, (maps, tall), 0)
    low = lax.broadcasted_iota(jnp.int32, (maps, tall), 1) < pairs
    sign = jnp.ones((maps, tall), jnp.float32)
    for h in range(group):
        sign = jnp.where(map_of == 2 * h + 1, jnp.where(low, -lam_own[h], -lam_own[group + h]), sign)

    row_of = lax.broadcasted_iota(jnp.int32, (2 * tall, keys), 0)
    col_of = lax.broadcasted_iota(jnp.int32, (2 * tall, keys), 1)
    query = 2 * pair + jnp.where(row_of < tall, row_of, row_of - tall)
    query = jnp.where(query >= tall, query - tall, query)
    place = jnp.where(
        col_of < key_dev,
        (2 * pair + core) * key_dev + col_of,
        (2 * pair + 1 - core) * key_dev + col_of - key_dev)
    bias[...] = jnp.where(place <= tall * key_dev - tall + query, 0.0, LOWEST)
    lane = lax.broadcasted_iota(jnp.int32, (tall, 128), 1)
    scaling = 1.0 / math.sqrt(128)

    for h in range(group):
        k_locals[h].wait()
        k_cross[h].wait_recv()
    all_of(q_wide.at[pl.ds(maps, (tall - 1) * maps)], qa_recv)

    stats = jnp.zeros((tall, 128), jnp.float32)
    expos = []
    blank = jnp.zeros((tall, 128), jnp.bfloat16)
    for h in range(group):
        first = q_wide[pl.ds(2 * h, tall, stride=maps), :].astype(jnp.bfloat16)
        second = q_wide[pl.ds(2 * h + 1, tall, stride=maps), :].astype(jnp.bfloat16)
        both = jnp.concatenate(
            [jnp.concatenate([first, blank], axis=1), jnp.concatenate([blank, second], axis=1)], axis=0)
        score = lax.dot_general(
            both, k_buf[h], (((1,), (1,)), ((), ())), preferred_element_type=jnp.float32)
        score = score * scaling + bias[...]
        top = jnp.max(score, axis=1, keepdims=True)
        expo = jnp.exp(score - top)
        total = jnp.sum(expo, axis=1, keepdims=True)
        for side in range(2):
            m = 2 * h + side
            at = slice(side * tall, (side + 1) * tall)
            stats = jnp.where(lane == m, top[at], jnp.where(lane == maps + m, total[at], stats))
        expos.append(expo.astype(jnp.bfloat16))
    stat_send[...] = stats

    def send_stats(t, where, its_core):
        pltpu.make_async_remote_copy(
            src_ref=stat_send.at[pl.ds(t, 1)], dst_ref=stat_recv.at[pl.ds(core * pairs + t // 2, 1)],
            send_sem=st_send, recv_sem=st_recv, device_id=where, device_id_type=MESH).start()

    def send_part(t, where, its_core):
        pltpu.make_async_remote_copy(
            src_ref=part_send.at[t], dst_ref=part_recv.at[t // 2 * 2 + core],
            send_sem=pa_send, recv_sem=pa_recv, device_id=where, device_id_type=MESH).start()

    to_all(send_stats)
    stat_recv[pl.ds(core * pairs, 1)] = stat_send[pl.ds(core, 1)]

    for h in range(group):
        v_locals[h].wait()
        v_cross[h].wait_recv()
    for h in range(group):
        summed = jnp.dot(expos[h], v_buf[h], preferred_element_type=jnp.float32)
        for side in range(2):
            for part in range(2):
                part_wide[pl.ds(part * maps + 2 * h + side, tall, stride=2 * maps), :] = summed[
                    side * tall : (side + 1) * tall, part * 128 : part * 128 + 128]
    part_send[...] = part_wide[...].reshape(tall, 2 * maps, 128).astype(jnp.bfloat16)
    to_all(send_part)
    part_recv[core] = part_send[core]

    all_of(stat_recv.at[pl.ds(1, tall - 1)], st_recv)
    turned = stat_recv[...].T
    tops, totals = turned[0:maps], turned[maps : 2 * maps]

    def per_group(array, reduce, fill):
        zero = reduce(jnp.where(low, array, fill), axis=1, keepdims=True)
        one = reduce(jnp.where(low, fill, array), axis=1, keepdims=True)
        return jnp.where(low, zero, one)

    factor = jnp.exp(tops - per_group(tops, jnp.max, -3e38))
    factor = factor * sign / per_group(factor * totals, jnp.sum, 0.0)
    gain_copy.wait()

    all_of(part_recv.at[pl.ds(1, tall - 1)], pa_recv)
    sums = [[jnp.zeros((maps, 128), jnp.float32) for _ in range(2)] for _ in range(2)]
    for s in range(pairs):
        for g in range(2):
            weight = factor[:, g * pairs + s : g * pairs + s + 1]
            block = part_recv[2 * s + g].astype(jnp.float32)
            for part in range(2):
                sums[part][g] = sums[part][g] + weight * block[part * maps : (part + 1) * maps]
    diffs = []
    for part in range(2):
        for g in range(2):
            sum_pad[part, g * maps : (g + 1) * maps] = sums[part][g]
        diffs.append(
            sum_pad[part, pl.ds(0, heads, stride=2), :] + sum_pad[part, pl.ds(1, heads, stride=2), :])
    square = jnp.sum(diffs[0] * diffs[0] + diffs[1] * diffs[1], axis=1, keepdims=True) * (1.0 / 256)
    scale = jnp.sqrt(square + 1e-05)
    normed = [diffs[part] / scale * gain_own[pl.ds(part, heads, stride=2), :] for part in range(2)]
    line = jnp.concatenate([normed[part][h : h + 1] for h in range(heads) for part in range(2)], axis=1)
    out_ref[...] = line.astype(jnp.bfloat16)

    for h in range(group):
        k_cross[h].wait_send()
        v_cross[h].wait_send()
    all_of(q_wide.at[pl.ds(maps, (tall - 1) * maps)], qa_send)
    all_of(stat_send.at[pl.ds(1, tall - 1)], st_send)
    all_of(part_send.at[pl.ds(1, tall - 1)], pa_send)


def shards(queries, key_maps, values, lambdas, norm_gain):
    rows, cols = lax.axis_size("qrow"), lax.axis_size("kcol")
    heads = lambdas.shape[0]
    key_dev = key_maps.shape[0]
    assert queries.shape[0] == 1 and heads == 8
    assert key_maps.shape[1] == 2048 and values.shape[1] == 2048
    assert cols % 2 == 0 and rows * cols <= 2 * key_dev
    group = heads // 2
    maps = 2 * group
    pairs = rows * cols // 2
    tall = 2 * pairs
    f32, bf16 = jnp.float32, jnp.bfloat16
    dma = pltpu.SemaphoreType.DMA
    in_hbm = pl.BlockSpec(memory_space=pltpu.HBM)
    out = pl.pallas_call(
        functools.partial(kernel, rows, cols, key_dev, heads),
        out_shape=jax.ShapeDtypeStruct((1, 2048), bf16),
        in_specs=[in_hbm] * 5,
        out_specs=pl.BlockSpec(memory_space=pltpu.VMEM),
        scratch_shapes=[
            pltpu.VMEM((1, 2048), bf16),
            pltpu.SMEM((heads,), f32),
            pltpu.VMEM((16, 128), f32),
            pltpu.VMEM((group, 2 * key_dev, 256), bf16),
            pltpu.VMEM((group, 2 * key_dev, 256), bf16),
            pltpu.VMEM((2, maps, 128), f32),
            pltpu.VMEM((pairs * 2 * maps, 128), f32),
            pltpu.VMEM((2 * tall, 2 * key_dev), f32),
            pltpu.VMEM((tall, 128), f32),
            pltpu.VMEM((tall, 128), f32),
            pltpu.VMEM((tall * 2 * maps, 128), f32),
            pltpu.VMEM((tall, 2 * maps, 128), bf16),
            pltpu.VMEM((tall, 2 * maps, 128), bf16),
            pltpu.VMEM((2, 2 * maps, 128), f32),
            dma, dma, dma,
            dma((group,)), dma((group,)), dma((group,)), dma((group,)), dma((group,)), dma((group,)),
            dma, dma, dma, dma, dma, dma,
        ],
        compiler_params=pltpu.CompilerParams(
            collective_id=0, has_side_effects=True),
        cost_estimate=pl.CostEstimate(
            flops=6 * tall * 2 * key_dev * 1024, bytes_accessed=4 * key_dev * 2048, transcendentals=0),
    )(queries, key_maps, values, lambdas, norm_gain.reshape(16, 128))
    return out


def solution(mesh):
    in_specs = (
        P(("qrow", "kcol"), None),
        P(("qrow", "kcol"), None),
        P(("qrow", "kcol"), None),
        P(),
        P(),
    )
    out_specs = P(("qrow", "kcol"), None)
    return jax.shard_map(shards, mesh=mesh, in_specs=in_specs, out_specs=out_specs, check_vma=False)
```

```python
import functools
import math

import jax
import jax.numpy as jnp
from jax import lax
from jax.experimental import pallas as pl
from jax.experimental.pallas import tpu as pltpu
from jax.sharding import PartitionSpec as P

MESH = pl.DeviceIdType.MESH
LOWEST = -1e30


def kernel(
    rows, cols, key_dev, heads,
    q_hbm, k_hbm, v_hbm, lam_hbm, gain_hbm,
    out_ref,
    q_own, lam_own, gain_own, k_buf, k_turned, v_buf, q_split, q_wide, bias,
    stat_send, stat_recv, part_wide, part_send, part_recv, sum_pad,
    q_sem, lam_sem, gain_sem, k_own_sem, v_own_sem, k_send, k_recv, v_send, v_recv,
    qa_send, qa_recv, st_send, st_recv, pa_send, pa_recv,
):
    row = lax.axis_index("qrow")
    col = lax.axis_index("kcol")
    core = lax.rem(col, 2)
    half_cols = cols // 2
    pairs = rows * half_cols
    pair = row * half_cols + lax.div(col, 2)
    sib = (row, col + 1 - 2 * core)
    group = heads // 2
    maps = 2 * group
    width = group * 256
    tall = 2 * pairs
    keys = 2 * key_dev

    def peer(offset, its_core):
        other = pair + offset
        other = jnp.where(other >= pairs, other - pairs, other)
        its_row = lax.div(other, half_cols)
        return (its_row, 2 * (other - its_row * half_cols) + its_core)

    def for_peers(step):
        if pairs <= 16:
            for i in range(1, pairs):
                step(i)
        else:
            lax.fori_loop(1, pairs, lambda i, carry: (step(i), carry)[1], 0)

    def columns(which, h):
        return pl.ds(pl.multiple_of(which * width + h * 256, 128), 256)

    def all_of(ref, sem):
        pltpu.make_async_copy(ref, ref, sem).wait()

    q_copy = pltpu.make_async_copy(q_hbm, q_own, q_sem)
    q_copy.start()
    barrier = pltpu.get_barrier_semaphore()

    def greet(i):
        for j in range(2):
            pl.semaphore_signal(barrier, inc=1, device_id=peer(i, j), device_id_type=MESH)

    pl.semaphore_signal(barrier, inc=1, device_id=sib, device_id_type=MESH)
    for_peers(greet)

    lam_copy = pltpu.make_async_copy(lam_hbm, lam_own, lam_sem)
    lam_copy.start()
    gain_copy = pltpu.make_async_copy(gain_hbm, gain_own, gain_sem)
    gain_copy.start()
    k_locals, v_locals = [], []
    for h in range(group):
        k_locals.append(pltpu.make_async_copy(
            k_hbm.at[:, columns(core, h)], k_buf.at[h, pl.ds(0, key_dev)], k_own_sem.at[h]))
        k_locals[-1].start()
    for h in range(group):
        v_locals.append(pltpu.make_async_copy(
            v_hbm.at[:, columns(core, h)], v_buf.at[h, pl.ds(0, key_dev)], v_own_sem.at[h]))
        v_locals[-1].start()

    q_copy.wait()
    for g in range(2):
        for m in range(maps):
            at = (g * maps + m) * 128
            q_split[g, m : m + 1, :] = q_own[:, at : at + 128].astype(jnp.float32)

    def to_all(send):
        for_peers(lambda i: [send(2 * i + j, peer(i, j), j) for j in range(2)])
        send(1 - core, sib, 1 - core)

    def send_query(t, where, its_core):
        back = lax.rem(tall - (t - its_core), tall) + core
        pltpu.make_async_remote_copy(
            src_ref=q_split.at[its_core], dst_ref=q_wide.at[pl.ds(pl.multiple_of(back * maps, 8), maps)],
            send_sem=qa_send, recv_sem=qa_recv, device_id=where, device_id_type=MESH).start()

    pl.semaphore_wait(barrier, tall - 1)

    to_all(send_query)
    q_wide[pl.ds(pl.multiple_of(core * maps, 8), maps)] = q_split[core]
    k_cross, v_cross = [], []
    for h in range(group):
        k_cross.append(pltpu.make_async_remote_copy(
            src_ref=k_hbm.at[:, columns(1 - core, h)], dst_ref=k_buf.at[h, pl.ds(key_dev, key_dev)],
            send_sem=k_send.at[h], recv_sem=k_recv.at[h], device_id=sib, device_id_type=MESH))
        k_cross[-1].start()

    for h in range(group):
        v_cross.append(pltpu.make_async_remote_copy(
            src_ref=v_hbm.at[:, columns(1 - core, h)], dst_ref=v_buf.at[h, pl.ds(key_dev, key_dev)],
            send_sem=v_send.at[h], recv_sem=v_recv.at[h], device_id=sib, device_id_type=MESH))
        v_cross[-1].start()

    lam_copy.wait()
    map_of = lax.broadcasted_iota(jnp.int32, (maps, tall), 0)
    low = lax.broadcasted_iota(jnp.int32, (maps, tall), 1) < pairs
    sign = jnp.ones((maps, tall), jnp.float32)
    for h in range(group):
        sign = jnp.where(map_of == 2 * h + 1, jnp.where(low, -lam_own[h], -lam_own[group + h]), sign)

    row_of = lax.broadcasted_iota(jnp.int32, (2 * tall, keys), 0)
    col_of = lax.broadcasted_iota(jnp.int32, (2 * tall, keys), 1)
    query = 2 * pair + jnp.where(row_of < tall, row_of, row_of - tall)
    query = jnp.where(query >= tall, query - tall, query)
    place = jnp.where(
        col_of < key_dev,
        (2 * pair + core) * key_dev + col_of,
        (2 * pair + 1 - core) * key_dev + col_of - key_dev)
    bias[...] = jnp.where(place <= tall * key_dev - tall + query, 0.0, LOWEST)
    lane = lax.broadcasted_iota(jnp.int32, (tall, 128), 1)
    scaling = 1.0 / math.sqrt(128)

    for h in range(group):
        k_locals[h].wait()
        k_turned[h, :, :key_dev] = k_buf[h, :key_dev].T
    for h in range(group):
        k_cross[h].wait_recv()
        k_turned[h, :, key_dev:] = k_buf[h, key_dev:].T
    all_of(q_wide.at[pl.ds(maps, (tall - 1) * maps)], qa_recv)

    stats = jnp.zeros((tall, 128), jnp.float32)
    expos = []
    blank = jnp.zeros((tall, 128), jnp.bfloat16)
    for h in range(group):
        first = q_wide[pl.ds(2 * h, tall, stride=maps), :].astype(jnp.bfloat16)
        second = q_wide[pl.ds(2 * h + 1, tall, stride=maps), :].astype(jnp.bfloat16)
        both = jnp.concatenate(
            [jnp.concatenate([first, blank], axis=1), jnp.concatenate([blank, second], axis=1)], axis=0)
        score = jnp.dot(both, k_turned[h], preferred_element_type=jnp.float32)
        score = score * scaling + bias[...]
        top = jnp.max(score, axis=1, keepdims=True)
        expo = jnp.exp(score - top)
        total = jnp.sum(expo, axis=1, keepdims=True)
        for side in range(2):
            m = 2 * h + side
            at = slice(side * tall, (side + 1) * tall)
            stats = jnp.where(lane == m, top[at], jnp.where(lane == maps + m, total[at], stats))
        expos.append(expo.astype(jnp.bfloat16))
    stat_send[...] = stats

    def send_stats(t, where, its_core):
        pltpu.make_async_remote_copy(
            src_ref=stat_send.at[pl.ds(t, 1)], dst_ref=stat_recv.at[pl.ds(core * pairs + t // 2, 1)],
            send_sem=st_send, recv_sem=st_recv, device_id=where, device_id_type=MESH).start()

    def send_part(t, where, its_core):
        pltpu.make_async_remote_copy(
            src_ref=part_send.at[t], dst_ref=part_recv.at[t // 2 * 2 + core],
            send_sem=pa_send, recv_sem=pa_recv, device_id=where, device_id_type=MESH).start()

    to_all(send_stats)
    stat_recv[pl.ds(core * pairs, 1)] = stat_send[pl.ds(core, 1)]

    for h in range(group):
        v_locals[h].wait()
        v_cross[h].wait_recv()
    for h in range(group):
        summed = jnp.dot(expos[h], v_buf[h], preferred_element_type=jnp.float32)
        for side in range(2):
            for part in range(2):
                part_wide[pl.ds(part * maps + 2 * h + side, tall, stride=2 * maps), :] = summed[
                    side * tall : (side + 1) * tall, part * 128 : part * 128 + 128]
    part_send[...] = part_wide[...].reshape(tall, 2 * maps, 128).astype(jnp.bfloat16)
    to_all(send_part)
    part_recv[core] = part_send[core]

    all_of(stat_recv.at[pl.ds(1, tall - 1)], st_recv)
    turned = stat_recv[...].T
    tops, totals = turned[0:maps], turned[maps : 2 * maps]

    def per_group(array, reduce, fill):
        zero = reduce(jnp.where(low, array, fill), axis=1, keepdims=True)
        one = reduce(jnp.where(low, fill, array), axis=1, keepdims=True)
        return jnp.where(low, zero, one)

    factor = jnp.exp(tops - per_group(tops, jnp.max, -3e38))
    factor = factor * sign / per_group(factor * totals, jnp.sum, 0.0)
    gain_copy.wait()

    all_of(part_recv.at[pl.ds(1, tall - 1)], pa_recv)
    sums = [[jnp.zeros((maps, 128), jnp.float32) for _ in range(2)] for _ in range(2)]
    for s in range(pairs):
        for g in range(2):
            weight = factor[:, g * pairs + s : g * pairs + s + 1]
            block = part_recv[2 * s + g].astype(jnp.float32)
            for part in range(2):
                sums[part][g] = sums[part][g] + weight * block[part * maps : (part + 1) * maps]
    diffs = []
    for part in range(2):
        for g in range(2):
            sum_pad[part, g * maps : (g + 1) * maps] = sums[part][g]
        diffs.append(
            sum_pad[part, pl.ds(0, heads, stride=2), :] + sum_pad[part, pl.ds(1, heads, stride=2), :])
    square = jnp.sum(diffs[0] * diffs[0] + diffs[1] * diffs[1], axis=1, keepdims=True) * (1.0 / 256)
    scale = jnp.sqrt(square + 1e-05)
    normed = [diffs[part] / scale * gain_own[pl.ds(part, heads, stride=2), :] for part in range(2)]
    line = jnp.concatenate([normed[part][h : h + 1] for h in range(heads) for part in range(2)], axis=1)
    out_ref[...] = line.astype(jnp.bfloat16)

    for h in range(group):
        k_cross[h].wait_send()
        v_cross[h].wait_send()
    all_of(q_wide.at[pl.ds(maps, (tall - 1) * maps)], qa_send)
    all_of(stat_send.at[pl.ds(1, tall - 1)], st_send)
    all_of(part_send.at[pl.ds(1, tall - 1)], pa_send)


def shards(queries, key_maps, values, lambdas, norm_gain):
    rows, cols = lax.axis_size("qrow"), lax.axis_size("kcol")
    heads = lambdas.shape[0]
    key_dev = key_maps.shape[0]
    assert queries.shape[0] == 1 and heads == 8
    assert key_maps.shape[1] == 2048 and values.shape[1] == 2048
    assert cols % 2 == 0 and rows * cols <= 2 * key_dev
    group = heads // 2
    maps = 2 * group
    pairs = rows * cols // 2
    tall = 2 * pairs
    f32, bf16 = jnp.float32, jnp.bfloat16
    dma = pltpu.SemaphoreType.DMA
    in_hbm = pl.BlockSpec(memory_space=pltpu.HBM)
    out = pl.pallas_call(
        functools.partial(kernel, rows, cols, key_dev, heads),
        out_shape=jax.ShapeDtypeStruct((1, 2048), bf16),
        in_specs=[in_hbm] * 5,
        out_specs=pl.BlockSpec(memory_space=pltpu.VMEM),
        scratch_shapes=[
            pltpu.VMEM((1, 2048), bf16),
            pltpu.SMEM((heads,), f32),
            pltpu.VMEM((16, 128), f32),
            pltpu.VMEM((group, 2 * key_dev, 256), bf16),
            pltpu.VMEM((group, 256, 2 * key_dev), bf16),
            pltpu.VMEM((group, 2 * key_dev, 256), bf16),
            pltpu.VMEM((2, maps, 128), f32),
            pltpu.VMEM((pairs * 2 * maps, 128), f32),
            pltpu.VMEM((2 * tall, 2 * key_dev), f32),
            pltpu.VMEM((tall, 128), f32),
            pltpu.VMEM((tall, 128), f32),
            pltpu.VMEM((tall * 2 * maps, 128), f32),
            pltpu.VMEM((tall, 2 * maps, 128), bf16),
            pltpu.VMEM((tall, 2 * maps, 128), bf16),
            pltpu.VMEM((2, 2 * maps, 128), f32),
            dma, dma, dma,
            dma((group,)), dma((group,)), dma((group,)), dma((group,)), dma((group,)), dma((group,)),
            dma, dma, dma, dma, dma, dma,
        ],
        compiler_params=pltpu.CompilerParams(
            collective_id=0, has_side_effects=True),
        cost_estimate=pl.CostEstimate(
            flops=6 * tall * 2 * key_dev * 1024, bytes_accessed=4 * key_dev * 2048, transcendentals=0),
    )(queries, key_maps, values, lambdas, norm_gain.reshape(16, 128))
    return out


def solution(mesh):
    in_specs = (
        P(("qrow", "kcol"), None),
        P(("qrow", "kcol"), None),
        P(("qrow", "kcol"), None),
        P(),
        P(),
    )
    out_specs = P(("qrow", "kcol"), None)
    return jax.shard_map(shards, mesh=mesh, in_specs=in_specs, out_specs=out_specs, check_vma=False)
```

```python
import functools
import math

import jax
import jax.numpy as jnp
from jax import lax
from jax.experimental import pallas as pl
from jax.experimental.pallas import tpu as pltpu
from jax.sharding import PartitionSpec as P

MESH = pl.DeviceIdType.MESH
LOWEST = -1e30


def kernel(
    rows, cols, key_dev, heads,
    q_hbm, k_hbm, v_hbm, lam_hbm, gain_hbm,
    out_ref,
    q_own, lam_own, gain_own, k_buf, v_buf, q_split, q_msg, q_in, q_wide, bias,
    stat_send, stat_recv, part_wide, part_send, part_recv, sum_pad,
    q_sem, lam_sem, gain_sem, k_own_sem, v_own_sem, k_send, k_recv, v_send, v_recv,
    qa_send, qa_recv, st_send, st_recv, pa_send, pa_recv,
):
    row = lax.axis_index("qrow")
    col = lax.axis_index("kcol")
    core = lax.rem(col, 2)
    half_cols = cols // 2
    pairs = rows * half_cols
    pair = row * half_cols + lax.div(col, 2)
    sib = (row, col + 1 - 2 * core)
    group = heads // 2
    maps = 2 * group
    width = group * 256
    tall = 2 * pairs
    keys = 2 * key_dev

    half = pairs // 2

    def apart(place):
        return (place & 3) + 8 * ((place >> 2) & (half // 4 - 1)) + 4 * (1 - place // half)

    def peer(place, its_core):
        other = pair ^ apart(place)
        its_row = lax.div(other, half_cols)
        return (its_row, 2 * (other - its_row * half_cols) + its_core)

    def to_far(send):
        if pairs <= 16:
            for place in range(half):
                for j in range(2):
                    send(place, j, peer(place, j))
        else:
            lax.fori_loop(0, half, lambda place, carry: ([
                send(place, j, peer(place, j)) for j in range(2)], carry)[1], 0)

    def to_near(send):
        if pairs <= 16:
            for place in range(half + 1, pairs):
                for j in range(2):
                    send(place, j, peer(place, j))
        else:
            lax.fori_loop(half + 1, pairs, lambda place, carry: ([
                send(place, j, peer(place, j)) for j in range(2)], carry)[1], 0)
        send(half, 1 - core, sib)

    def columns(which, h):
        return pl.ds(pl.multiple_of(which * width + h * 256, 128), 256)

    def all_of(ref, sem):
        pltpu.make_async_copy(ref, ref, sem).wait()

    q_copy = pltpu.make_async_copy(q_hbm, q_own, q_sem)
    q_copy.start()
    barrier = pltpu.get_barrier_semaphore()

    def greet(place, j, where):
        pl.semaphore_signal(barrier, inc=1, device_id=where, device_id_type=MESH)

    to_far(greet)
    to_near(greet)

    lam_copy = pltpu.make_async_copy(lam_hbm, lam_own, lam_sem)
    lam_copy.start()
    gain_copy = pltpu.make_async_copy(gain_hbm, gain_own, gain_sem)
    gain_copy.start()
    k_locals, v_locals = [], []
    for h in range(group):
        k_locals.append(pltpu.make_async_copy(
            k_hbm.at[:, columns(core, h)], k_buf.at[h, pl.ds(0, key_dev)], k_own_sem.at[h]))
        k_locals[-1].start()
    for h in range(group):
        v_locals.append(pltpu.make_async_copy(
            v_hbm.at[:, columns(core, h)], v_buf.at[h, pl.ds(0, key_dev)], v_own_sem.at[h]))
        v_locals[-1].start()

    q_copy.wait()
    for g in range(2):
        for m in range(maps):
            at = (g * maps + m) * 128
            q_split[g, m : m + 1, :] = q_own[:, at : at + 128].astype(jnp.float32)

    q_msg[...] = q_split[...].astype(jnp.bfloat16)

    def send_query(place, j, where):
        pltpu.make_async_remote_copy(
            src_ref=q_msg.at[j], dst_ref=q_in.at[2 * place + core],
            send_sem=qa_send, recv_sem=qa_recv, device_id=where, device_id_type=MESH).start()

    pl.semaphore_wait(barrier, tall - 1)

    to_far(send_query)
    to_near(send_query)
    q_in[2 * half + core] = q_msg[core]
    k_cross, v_cross = [], []
    for h in range(group):
        k_cross.append(pltpu.make_async_remote_copy(
            src_ref=k_hbm.at[:, columns(1 - core, h)], dst_ref=k_buf.at[h, pl.ds(key_dev, key_dev)],
            send_sem=k_send.at[h], recv_sem=k_recv.at[h], device_id=sib, device_id_type=MESH))
        k_cross[-1].start()

    for h in range(group):
        v_cross.append(pltpu.make_async_remote_copy(
            src_ref=v_hbm.at[:, columns(1 - core, h)], dst_ref=v_buf.at[h, pl.ds(key_dev, key_dev)],
            send_sem=v_send.at[h], recv_sem=v_recv.at[h], device_id=sib, device_id_type=MESH))
        v_cross[-1].start()

    lam_copy.wait()
    map_of = lax.broadcasted_iota(jnp.int32, (maps, tall), 0)
    low = lax.broadcasted_iota(jnp.int32, (maps, tall), 1) < pairs
    sign = jnp.ones((maps, tall), jnp.float32)
    for h in range(group):
        sign = jnp.where(map_of == 2 * h + 1, jnp.where(low, -lam_own[h], -lam_own[group + h]), sign)

    row_of = lax.broadcasted_iota(jnp.int32, (2 * tall, keys), 0)
    col_of = lax.broadcasted_iota(jnp.int32, (2 * tall, keys), 1)
    row_of = row_of & (tall - 1)
    row_place = row_of >> 1
    row_apart = (row_place & 3) + 8 * ((row_place >> 2) & (half // 4 - 1)) + jnp.where(row_place < half, 4, 0)
    query = 2 * (pair ^ row_apart) + (row_of & 1)
    place = jnp.where(
        col_of < key_dev,
        (2 * pair + core) * key_dev + col_of,
        (2 * pair + 1 - core) * key_dev + col_of - key_dev)
    bias[...] = jnp.where(place <= tall * key_dev - tall + query, 0.0, LOWEST)
    lane = lax.broadcasted_iota(jnp.int32, (tall, 128), 1)
    scaling = 1.0 / math.sqrt(128)

    for h in range(group):
        k_locals[h].wait()
        k_cross[h].wait_recv()
    all_of(q_in.at[pl.ds(1, tall - 1)], qa_recv)
    q_wide[...] = q_in[...].astype(jnp.float32).reshape(tall * maps, 128)

    stats = jnp.zeros((tall, 128), jnp.float32)
    expos = []
    blank = jnp.zeros((tall, 128), jnp.bfloat16)
    for h in range(group):
        first = q_wide[pl.ds(2 * h, tall, stride=maps), :].astype(jnp.bfloat16)
        second = q_wide[pl.ds(2 * h + 1, tall, stride=maps), :].astype(jnp.bfloat16)
        both = jnp.concatenate(
            [jnp.concatenate([first, blank], axis=1), jnp.concatenate([blank, second], axis=1)], axis=0)
        score = lax.dot_general(
            both, k_buf[h], (((1,), (1,)), ((), ())), preferred_element_type=jnp.float32)
        score = score * scaling + bias[...]
        top = jnp.max(score, axis=1, keepdims=True)
        expo = jnp.exp(score - top)
        total = jnp.sum(expo, axis=1, keepdims=True)
        for side in range(2):
            m = 2 * h + side
            at = slice(side * tall, (side + 1) * tall)
            stats = jnp.where(lane == m, top[at], jnp.where(lane == maps + m, total[at], stats))
        expos.append(expo.astype(jnp.bfloat16))
    stat_send[...] = stats

    def send_stats(place, j, where):
        pltpu.make_async_remote_copy(
            src_ref=stat_send.at[pl.ds(2 * place + j, 1)], dst_ref=stat_recv.at[pl.ds(core * pairs + place, 1)],
            send_sem=st_send, recv_sem=st_recv, device_id=where, device_id_type=MESH).start()

    def send_part(place, j, where):
        pltpu.make_async_remote_copy(
            src_ref=part_send.at[2 * place + j], dst_ref=part_recv.at[2 * place + core],
            send_sem=pa_send, recv_sem=pa_recv, device_id=where, device_id_type=MESH).start()

    def weigh(start):
        for h in range(group):
            rows_of = jnp.concatenate([expos[h][start : start + pairs], expos[h][tall + start : tall + start + pairs]], axis=0)
            summed = jnp.dot(rows_of, v_buf[h], preferred_element_type=jnp.float32)
            for side in range(2):
                for part in range(2):
                    at = pl.ds(start * 2 * maps + part * maps + 2 * h + side, pairs, stride=2 * maps)
                    part_wide[at, :] = summed[side * pairs : (side + 1) * pairs, part * 128 : part * 128 + 128]
        part_send[start : start + pairs] = part_wide[start * 2 * maps : (start + pairs) * 2 * maps].reshape(
            pairs, 2 * maps, 128).astype(jnp.bfloat16)

    for h in range(group):
        v_locals[h].wait()
        v_cross[h].wait_recv()
    weigh(0)
    to_far(send_part)
    to_far(send_stats)
    to_near(send_stats)
    stat_recv[pl.ds(core * pairs + half, 1)] = stat_send[pl.ds(2 * half + core, 1)]
    weigh(pairs)
    to_near(send_part)
    part_recv[2 * half + core] = part_send[2 * half + core]

    all_of(stat_recv.at[pl.ds(1, tall - 1)], st_recv)
    turned = stat_recv[...].T
    tops, totals = turned[0:maps], turned[maps : 2 * maps]

    def per_group(array, reduce, fill):
        zero = reduce(jnp.where(low, array, fill), axis=1, keepdims=True)
        one = reduce(jnp.where(low, fill, array), axis=1, keepdims=True)
        return jnp.where(low, zero, one)

    factor = jnp.exp(tops - per_group(tops, jnp.max, -3e38))
    factor = factor * sign / per_group(factor * totals, jnp.sum, 0.0)
    gain_copy.wait()

    all_of(part_recv.at[pl.ds(1, tall - 1)], pa_recv)
    sums = [[jnp.zeros((maps, 128), jnp.float32) for _ in range(2)] for _ in range(2)]
    for s in range(pairs):
        for g in range(2):
            weight = factor[:, g * pairs + s : g * pairs + s + 1]
            block = part_recv[2 * s + g].astype(jnp.float32)
            for part in range(2):
                sums[part][g] = sums[part][g] + weight * block[part * maps : (part + 1) * maps]
    diffs = []
    for part in range(2):
        for g in range(2):
            sum_pad[part, g * maps : (g + 1) * maps] = sums[part][g]
        diffs.append(
            sum_pad[part, pl.ds(0, heads, stride=2), :] + sum_pad[part, pl.ds(1, heads, stride=2), :])
    square = jnp.sum(diffs[0] * diffs[0] + diffs[1] * diffs[1], axis=1, keepdims=True) * (1.0 / 256)
    scale = jnp.sqrt(square + 1e-05)
    normed = [diffs[part] / scale * gain_own[pl.ds(part, heads, stride=2), :] for part in range(2)]
    line = jnp.concatenate([normed[part][h : h + 1] for h in range(heads) for part in range(2)], axis=1)
    out_ref[...] = line.astype(jnp.bfloat16)

    for h in range(group):
        k_cross[h].wait_send()
        v_cross[h].wait_send()
    all_of(q_in.at[pl.ds(1, tall - 1)], qa_send)
    all_of(stat_send.at[pl.ds(1, tall - 1)], st_send)
    all_of(part_send.at[pl.ds(1, tall - 1)], pa_send)


def shards(queries, key_maps, values, lambdas, norm_gain):
    rows, cols = lax.axis_size("qrow"), lax.axis_size("kcol")
    heads = lambdas.shape[0]
    key_dev = key_maps.shape[0]
    assert queries.shape[0] == 1 and heads == 8
    assert key_maps.shape[1] == 2048 and values.shape[1] == 2048
    assert cols % 2 == 0 and rows * cols >= 16 and (rows * cols) & (rows * cols - 1) == 0
    assert rows * cols <= 2 * key_dev
    group = heads // 2
    maps = 2 * group
    pairs = rows * cols // 2
    tall = 2 * pairs
    f32, bf16 = jnp.float32, jnp.bfloat16
    dma = pltpu.SemaphoreType.DMA
    in_hbm = pl.BlockSpec(memory_space=pltpu.HBM)
    out = pl.pallas_call(
        functools.partial(kernel, rows, cols, key_dev, heads),
        out_shape=jax.ShapeDtypeStruct((1, 2048), bf16),
        in_specs=[in_hbm] * 5,
        out_specs=pl.BlockSpec(memory_space=pltpu.VMEM),
        scratch_shapes=[
            pltpu.VMEM((1, 2048), bf16),
            pltpu.SMEM((heads,), f32),
            pltpu.VMEM((16, 128), f32),
            pltpu.VMEM((group, 2 * key_dev, 256), bf16),
            pltpu.VMEM((group, 2 * key_dev, 256), bf16),
            pltpu.VMEM((2, maps, 128), f32),
            pltpu.VMEM((2, maps, 128), bf16),
            pltpu.VMEM((tall, maps, 128), bf16),
            pltpu.VMEM((tall * maps, 128), f32),
            pltpu.VMEM((2 * tall, 2 * key_dev), f32),
            pltpu.VMEM((tall, 128), f32),
            pltpu.VMEM((tall, 128), f32),
            pltpu.VMEM((tall * 2 * maps, 128), f32),
            pltpu.VMEM((tall, 2 * maps, 128), bf16),
            pltpu.VMEM((tall, 2 * maps, 128), bf16),
            pltpu.VMEM((2, 2 * maps, 128), f32),
            dma, dma, dma,
            dma((group,)), dma((group,)), dma((group,)), dma((group,)), dma((group,)), dma((group,)),
            dma, dma, dma, dma, dma, dma,
        ],
        compiler_params=pltpu.CompilerParams(
            collective_id=0, has_side_effects=True),
        cost_estimate=pl.CostEstimate(
            flops=6 * tall * 2 * key_dev * 1024, bytes_accessed=4 * key_dev * 2048, transcendentals=0),
    )(queries, key_maps, values, lambdas, norm_gain.reshape(16, 128))
    return out


def solution(mesh):
    in_specs = (
        P(("qrow", "kcol"), None),
        P(("qrow", "kcol"), None),
        P(("qrow", "kcol"), None),
        P(),
        P(),
    )
    out_specs = P(("qrow", "kcol"), None)
    return jax.shard_map(shards, mesh=mesh, in_specs=in_specs, out_specs=out_specs, check_vma=False)
```

```python
import functools
import math

import jax
import jax.numpy as jnp
from jax import lax
from jax.experimental import pallas as pl
from jax.experimental.pallas import tpu as pltpu
from jax.sharding import PartitionSpec as P

MESH = pl.DeviceIdType.MESH
LOWEST = -1e30


def kernel(
    rows, cols, key_dev, heads,
    q_hbm, k_hbm, v_hbm, lam_hbm, gain_hbm,
    out_ref,
    q_own, lam_own, gain_own, k_buf, v_buf, q_split, q_msg, q_in, q_wide, bias,
    stat_send, stat_recv, part_wide, part_send, part_recv, sum_pad,
    q_sem, lam_sem, gain_sem, k_own_sem, v_own_sem, k_send, k_recv, v_send, v_recv,
    qa_send, qa_recv, st_send, st_recv, pa_send, pa_recv,
):
    row = lax.axis_index("qrow")
    col = lax.axis_index("kcol")
    core = lax.rem(col, 2)
    half_cols = cols // 2
    pairs = rows * half_cols
    pair = row * half_cols + lax.div(col, 2)
    sib = (row, col + 1 - 2 * core)
    group = heads // 2
    maps = 2 * group
    width = group * 256
    tall = 2 * pairs
    keys = 2 * key_dev

    def peer(offset, its_core):
        other = pair + offset
        other = jnp.where(other >= pairs, other - pairs, other)
        its_row = lax.div(other, half_cols)
        return (its_row, 2 * (other - its_row * half_cols) + its_core)

    def for_peers(step):
        if pairs <= 16:
            for i in range(1, pairs):
                step(i)
        else:
            lax.fori_loop(1, pairs, lambda i, carry: (step(i), carry)[1], 0)

    def columns(which, h):
        return pl.ds(pl.multiple_of(which * width + h * 256, 128), 256)

    def all_of(ref, sem):
        pltpu.make_async_copy(ref, ref, sem).wait()

    q_copy = pltpu.make_async_copy(q_hbm, q_own, q_sem)
    q_copy.start()
    barrier = pltpu.get_barrier_semaphore()

    def greet(i):
        for j in range(2):
            pl.semaphore_signal(barrier, inc=1, device_id=peer(i, j), device_id_type=MESH)

    pl.semaphore_signal(barrier, inc=1, device_id=sib, device_id_type=MESH)
    for_peers(greet)

    lam_copy = pltpu.make_async_copy(lam_hbm, lam_own, lam_sem)
    lam_copy.start()
    gain_copy = pltpu.make_async_copy(gain_hbm, gain_own, gain_sem)
    gain_copy.start()
    k_locals, v_locals = [], []
    for h in range(group):
        k_locals.append(pltpu.make_async_copy(
            k_hbm.at[:, columns(core, h)], k_buf.at[h, pl.ds(0, key_dev)], k_own_sem.at[h]))
        k_locals[-1].start()
    for h in range(group):
        v_locals.append(pltpu.make_async_copy(
            v_hbm.at[:, columns(core, h)], v_buf.at[h, pl.ds(0, key_dev)], v_own_sem.at[h]))
        v_locals[-1].start()

    q_copy.wait()
    for g in range(2):
        for m in range(maps):
            at = (g * maps + m) * 128
            q_split[g, m : m + 1, :] = q_own[:, at : at + 128].astype(jnp.float32)

    q_msg[...] = q_split[...].astype(jnp.bfloat16)

    def to_all(send):
        for_peers(lambda i: [send(2 * i + j, peer(i, j), j) for j in range(2)])
        send(1 - core, sib, 1 - core)

    def send_query(t, where, its_core):
        back = lax.rem(tall - (t - its_core), tall) + core
        pltpu.make_async_remote_copy(
            src_ref=q_msg.at[its_core], dst_ref=q_in.at[back],
            send_sem=qa_send, recv_sem=qa_recv, device_id=where, device_id_type=MESH).start()

    pl.semaphore_wait(barrier, tall - 1)

    to_all(send_query)
    q_in[core] = q_msg[core]
    k_cross, v_cross = [], []
    for h in range(group):
        k_cross.append(pltpu.make_async_remote_copy(
            src_ref=k_hbm.at[:, columns(1 - core, h)], dst_ref=k_buf.at[h, pl.ds(key_dev, key_dev)],
            send_sem=k_send.at[h], recv_sem=k_recv.at[h], device_id=sib, device_id_type=MESH))
        k_cross[-1].start()

    for h in range(group):
        v_cross.append(pltpu.make_async_remote_copy(
            src_ref=v_hbm.at[:, columns(1 - core, h)], dst_ref=v_buf.at[h, pl.ds(key_dev, key_dev)],
            send_sem=v_send.at[h], recv_sem=v_recv.at[h], device_id=sib, device_id_type=MESH))
        v_cross[-1].start()

    lam_copy.wait()
    map_of = lax.broadcasted_iota(jnp.int32, (maps, tall), 0)
    low = lax.broadcasted_iota(jnp.int32, (maps, tall), 1) < pairs
    sign = jnp.ones((maps, tall), jnp.float32)
    for h in range(group):
        sign = jnp.where(map_of == 2 * h + 1, jnp.where(low, -lam_own[h], -lam_own[group + h]), sign)

    row_of = lax.broadcasted_iota(jnp.int32, (2 * tall, keys), 0)
    col_of = lax.broadcasted_iota(jnp.int32, (2 * tall, keys), 1)
    query = 2 * pair + jnp.where(row_of < tall, row_of, row_of - tall)
    query = jnp.where(query >= tall, query - tall, query)
    place = jnp.where(
        col_of < key_dev,
        (2 * pair + core) * key_dev + col_of,
        (2 * pair + 1 - core) * key_dev + col_of - key_dev)
    bias[...] = jnp.where(place <= tall * key_dev - tall + query, 0.0, LOWEST)
    lane = lax.broadcasted_iota(jnp.int32, (tall, 128), 1)
    scaling = 1.0 / math.sqrt(128)

    for h in range(group):
        k_locals[h].wait()
        k_cross[h].wait_recv()
    all_of(q_in.at[pl.ds(1, tall - 1)], qa_recv)
    q_wide[...] = q_in[...].astype(jnp.float32).reshape(tall * maps, 128)

    stats = jnp.zeros((tall, 128), jnp.float32)
    expos = []
    blank = jnp.zeros((tall, 128), jnp.bfloat16)
    for h in range(group):
        first = q_wide[pl.ds(2 * h, tall, stride=maps), :].astype(jnp.bfloat16)
        second = q_wide[pl.ds(2 * h + 1, tall, stride=maps), :].astype(jnp.bfloat16)
        both = jnp.concatenate(
            [jnp.concatenate([first, blank], axis=1), jnp.concatenate([blank, second], axis=1)], axis=0)
        score = lax.dot_general(
            both, k_buf[h], (((1,), (1,)), ((), ())), preferred_element_type=jnp.float32)
        score = score * scaling + bias[...]
        top = jnp.max(score, axis=1, keepdims=True)
        expo = jnp.exp(score - top)
        total = jnp.sum(expo, axis=1, keepdims=True)
        for side in range(2):
            m = 2 * h + side
            at = slice(side * tall, (side + 1) * tall)
            stats = jnp.where(lane == m, top[at], jnp.where(lane == maps + m, total[at], stats))
        expos.append(expo.astype(jnp.bfloat16))
    stat_send[...] = stats

    def send_stats(t, where, its_core):
        pltpu.make_async_remote_copy(
            src_ref=stat_send.at[pl.ds(t, 1)], dst_ref=stat_recv.at[pl.ds(core * pairs + t // 2, 1)],
            send_sem=st_send, recv_sem=st_recv, device_id=where, device_id_type=MESH).start()

    def send_part(t, where, its_core):
        pltpu.make_async_remote_copy(
            src_ref=part_send.at[t], dst_ref=part_recv.at[t // 2 * 2 + core],
            send_sem=pa_send, recv_sem=pa_recv, device_id=where, device_id_type=MESH).start()

    to_all(send_stats)
    stat_recv[pl.ds(core * pairs, 1)] = stat_send[pl.ds(core, 1)]

    for h in range(group):
        v_locals[h].wait()
        v_cross[h].wait_recv()
    for h in range(group):
        summed = jnp.dot(expos[h], v_buf[h], preferred_element_type=jnp.float32)
        for side in range(2):
            for part in range(2):
                part_wide[pl.ds(part * maps + 2 * h + side, tall, stride=2 * maps), :] = summed[
                    side * tall : (side + 1) * tall, part * 128 : part * 128 + 128]
    part_send[...] = part_wide[...].reshape(tall, 2 * maps, 128).astype(jnp.bfloat16)
    to_all(send_part)
    part_recv[core] = part_send[core]

    all_of(stat_recv.at[pl.ds(1, tall - 1)], st_recv)
    turned = stat_recv[...].T
    tops, totals = turned[0:maps], turned[maps : 2 * maps]

    def per_group(array, reduce, fill):
        zero = reduce(jnp.where(low, array, fill), axis=1, keepdims=True)
        one = reduce(jnp.where(low, fill, array), axis=1, keepdims=True)
        return jnp.where(low, zero, one)

    factor = jnp.exp(tops - per_group(tops, jnp.max, -3e38))
    factor = factor * sign / per_group(factor * totals, jnp.sum, 0.0)
    gain_copy.wait()

    all_of(part_recv.at[pl.ds(1, tall - 1)], pa_recv)
    sums = [[jnp.zeros((maps, 128), jnp.float32) for _ in range(2)] for _ in range(2)]
    for s in range(pairs):
        for g in range(2):
            weight = factor[:, g * pairs + s : g * pairs + s + 1]
            block = part_recv[2 * s + g].astype(jnp.float32)
            for part in range(2):
                sums[part][g] = sums[part][g] + weight * block[part * maps : (part + 1) * maps]
    diffs = []
    for part in range(2):
        for g in range(2):
            sum_pad[part, g * maps : (g + 1) * maps] = sums[part][g]
        diffs.append(
            sum_pad[part, pl.ds(0, heads, stride=2), :] + sum_pad[part, pl.ds(1, heads, stride=2), :])
    square = jnp.sum(diffs[0] * diffs[0] + diffs[1] * diffs[1], axis=1, keepdims=True) * (1.0 / 256)
    scale = jnp.sqrt(square + 1e-05)
    normed = [diffs[part] / scale * gain_own[pl.ds(part, heads, stride=2), :] for part in range(2)]
    line = jnp.concatenate([normed[part][h : h + 1] for h in range(heads) for part in range(2)], axis=1)
    out_ref[...] = line.astype(jnp.bfloat16)

    for h in range(group):
        k_cross[h].wait_send()
        v_cross[h].wait_send()
    all_of(q_in.at[pl.ds(1, tall - 1)], qa_send)
    all_of(stat_send.at[pl.ds(1, tall - 1)], st_send)
    all_of(part_send.at[pl.ds(1, tall - 1)], pa_send)


def shards(queries, key_maps, values, lambdas, norm_gain):
    rows, cols = lax.axis_size("qrow"), lax.axis_size("kcol")
    heads = lambdas.shape[0]
    key_dev = key_maps.shape[0]
    assert queries.shape[0] == 1 and heads == 8
    assert key_maps.shape[1] == 2048 and values.shape[1] == 2048
    assert cols % 2 == 0 and rows * cols <= 2 * key_dev
    group = heads // 2
    maps = 2 * group
    pairs = rows * cols // 2
    tall = 2 * pairs
    f32, bf16 = jnp.float32, jnp.bfloat16
    dma = pltpu.SemaphoreType.DMA
    in_hbm = pl.BlockSpec(memory_space=pltpu.HBM)
    out = pl.pallas_call(
        functools.partial(kernel, rows, cols, key_dev, heads),
        out_shape=jax.ShapeDtypeStruct((1, 2048), bf16),
        in_specs=[in_hbm] * 5,
        out_specs=pl.BlockSpec(memory_space=pltpu.VMEM),
        scratch_shapes=[
            pltpu.VMEM((1, 2048), bf16),
            pltpu.SMEM((heads,), f32),
            pltpu.VMEM((16, 128), f32),
            pltpu.VMEM((group, 2 * key_dev, 256), bf16),
            pltpu.VMEM((group, 2 * key_dev, 256), bf16),
            pltpu.VMEM((2, maps, 128), f32),
            pltpu.VMEM((2, maps, 128), bf16),
            pltpu.VMEM((tall, maps, 128), bf16),
            pltpu.VMEM((tall * maps, 128), f32),
            pltpu.VMEM((2 * tall, 2 * key_dev), f32),
            pltpu.VMEM((tall, 128), f32),
            pltpu.VMEM((tall, 128), f32),
            pltpu.VMEM((tall * 2 * maps, 128), f32),
            pltpu.VMEM((tall, 2 * maps, 128), bf16),
            pltpu.VMEM((tall, 2 * maps, 128), bf16),
            pltpu.VMEM((2, 2 * maps, 128), f32),
            dma, dma, dma,
            dma((group,)), dma((group,)), dma((group,)), dma((group,)), dma((group,)), dma((group,)),
            dma, dma, dma, dma, dma, dma,
        ],
        compiler_params=pltpu.CompilerParams(
            collective_id=0, has_side_effects=True),
        cost_estimate=pl.CostEstimate(
            flops=6 * tall * 2 * key_dev * 1024, bytes_accessed=4 * key_dev * 2048, transcendentals=0),
    )(queries, key_maps, values, lambdas, norm_gain.reshape(16, 128))
    return out


def solution(mesh):
    in_specs = (
        P(("qrow", "kcol"), None),
        P(("qrow", "kcol"), None),
        P(("qrow", "kcol"), None),
        P(),
        P(),
    )
    out_specs = P(("qrow", "kcol"), None)
    return jax.shard_map(shards, mesh=mesh, in_specs=in_specs, out_specs=out_specs, check_vma=False)
```

```python
import functools
import math

import jax
import jax.numpy as jnp
from jax import lax
from jax.experimental import pallas as pl
from jax.experimental.pallas import tpu as pltpu
from jax.sharding import PartitionSpec as P

MESH = pl.DeviceIdType.MESH
LOWEST = -1e30


def kernel(
    rows, cols, key_dev, heads,
    q_hbm, k_hbm, v_hbm, lam_hbm,
    out_ref,
    q_own, lam_own, k_buf, v_buf, q_split, q_msg, q_in, q_wide, bias,
    stat_send, stat_recv, part_wide, part_send, part_recv, sum_pad,
    q_sem, lam_sem, k_own_sem, v_own_sem, k_send, k_recv, v_send, v_recv,
    qa_send, qa_recv, st_send, st_recv, pa_send, pa_recv,
):
    row = lax.axis_index("qrow")
    col = lax.axis_index("kcol")
    core = lax.rem(col, 2)
    half_cols = cols // 2
    pairs = rows * half_cols
    pair = row * half_cols + lax.div(col, 2)
    sib = (row, col + 1 - 2 * core)
    group = heads // 2
    maps = 2 * group
    width = group * 256
    tall = 2 * pairs
    keys = 2 * key_dev

    def peer(offset, its_core):
        other = pair + offset
        other = jnp.where(other >= pairs, other - pairs, other)
        its_row = lax.div(other, half_cols)
        return (its_row, 2 * (other - its_row * half_cols) + its_core)

    def for_peers(step):
        if pairs <= 16:
            for i in range(1, pairs):
                step(i)
        else:
            lax.fori_loop(1, pairs, lambda i, carry: (step(i), carry)[1], 0)

    def columns(which, h):
        return pl.ds(pl.multiple_of(which * width + h * 256, 128), 256)

    def all_of(ref, sem):
        pltpu.make_async_copy(ref, ref, sem).wait()

    q_copy = pltpu.make_async_copy(q_hbm, q_own, q_sem)
    q_copy.start()
    barrier = pltpu.get_barrier_semaphore()

    def greet(i):
        for j in range(2):
            pl.semaphore_signal(barrier, inc=1, device_id=peer(i, j), device_id_type=MESH)

    pl.semaphore_signal(barrier, inc=1, device_id=sib, device_id_type=MESH)
    for_peers(greet)

    lam_copy = pltpu.make_async_copy(lam_hbm, lam_own, lam_sem)
    lam_copy.start()
    k_locals, v_locals = [], []
    for h in range(group):
        k_locals.append(pltpu.make_async_copy(
            k_hbm.at[:, columns(core, h)], k_buf.at[h, pl.ds(0, key_dev)], k_own_sem.at[h]))
        k_locals[-1].start()
    for h in range(group):
        v_locals.append(pltpu.make_async_copy(
            v_hbm.at[:, columns(core, h)], v_buf.at[h, pl.ds(0, key_dev)], v_own_sem.at[h]))
        v_locals[-1].start()

    q_copy.wait()
    for g in range(2):
        for m in range(maps):
            at = (g * maps + m) * 128
            q_split[g, m : m + 1, :] = q_own[:, at : at + 128].astype(jnp.float32)

    q_msg[...] = q_split[...].astype(jnp.bfloat16)

    def to_all(send):
        for_peers(lambda i: [send(2 * i + j, peer(i, j), j) for j in range(2)])
        send(1 - core, sib, 1 - core)

    def send_query(t, where, its_core):
        back = lax.rem(tall - (t - its_core), tall) + core
        pltpu.make_async_remote_copy(
            src_ref=q_msg.at[its_core], dst_ref=q_in.at[back],
            send_sem=qa_send, recv_sem=qa_recv, device_id=where, device_id_type=MESH).start()

    pl.semaphore_wait(barrier, tall - 1)

    to_all(send_query)
    q_in[core] = q_msg[core]
    k_cross, v_cross = [], []
    for h in range(group):
        k_cross.append(pltpu.make_async_remote_copy(
            src_ref=k_hbm.at[:, columns(1 - core, h)], dst_ref=k_buf.at[h, pl.ds(key_dev, key_dev)],
            send_sem=k_send.at[h], recv_sem=k_recv.at[h], device_id=sib, device_id_type=MESH))
        k_cross[-1].start()

    for h in range(group):
        v_cross.append(pltpu.make_async_remote_copy(
            src_ref=v_hbm.at[:, columns(1 - core, h)], dst_ref=v_buf.at[h, pl.ds(key_dev, key_dev)],
            send_sem=v_send.at[h], recv_sem=v_recv.at[h], device_id=sib, device_id_type=MESH))
        v_cross[-1].start()

    lam_copy.wait()
    map_of = lax.broadcasted_iota(jnp.int32, (maps, tall), 0)
    low = lax.broadcasted_iota(jnp.int32, (maps, tall), 1) < pairs
    sign = jnp.ones((maps, tall), jnp.float32)
    for h in range(group):
        sign = jnp.where(map_of == 2 * h + 1, jnp.where(low, -lam_own[h], -lam_own[group + h]), sign)

    row_of = lax.broadcasted_iota(jnp.int32, (2 * tall, keys), 0)
    col_of = lax.broadcasted_iota(jnp.int32, (2 * tall, keys), 1)
    query = 2 * pair + jnp.where(row_of < tall, row_of, row_of - tall)
    query = jnp.where(query >= tall, query - tall, query)
    place = jnp.where(
        col_of < key_dev,
        (2 * pair + core) * key_dev + col_of,
        (2 * pair + 1 - core) * key_dev + col_of - key_dev)
    bias[...] = jnp.where(place <= tall * key_dev - tall + query, 0.0, LOWEST)
    lane = lax.broadcasted_iota(jnp.int32, (tall, 128), 1)
    scaling = 1.0 / math.sqrt(128)

    for h in range(group):
        k_locals[h].wait()
        k_cross[h].wait_recv()
    all_of(q_in.at[pl.ds(1, tall - 1)], qa_recv)
    q_wide[...] = q_in[...].astype(jnp.float32).reshape(tall * maps, 128)

    stats = jnp.zeros((tall, 128), jnp.float32)
    expos = []
    blank = jnp.zeros((tall, 128), jnp.bfloat16)
    for h in range(group):
        first = q_wide[pl.ds(2 * h, tall, stride=maps), :].astype(jnp.bfloat16)
        second = q_wide[pl.ds(2 * h + 1, tall, stride=maps), :].astype(jnp.bfloat16)
        both = jnp.concatenate(
            [jnp.concatenate([first, blank], axis=1), jnp.concatenate([blank, second], axis=1)], axis=0)
        score = lax.dot_general(
            both, k_buf[h], (((1,), (1,)), ((), ())), preferred_element_type=jnp.float32)
        score = score * scaling + bias[...]
        top = jnp.max(score, axis=1, keepdims=True)
        expo = jnp.exp(score - top)
        total = jnp.sum(expo, axis=1, keepdims=True)
        for side in range(2):
            m = 2 * h + side
            at = slice(side * tall, (side + 1) * tall)
            stats = jnp.where(lane == m, top[at], jnp.where(lane == maps + m, total[at], stats))
        expos.append(expo.astype(jnp.bfloat16))
    stat_send[...] = stats

    def send_stats(t, where, its_core):
        pltpu.make_async_remote_copy(
            src_ref=stat_send.at[pl.ds(t, 1)], dst_ref=stat_recv.at[pl.ds(core * pairs + t // 2, 1)],
            send_sem=st_send, recv_sem=st_recv, device_id=where, device_id_type=MESH).start()

    def send_part(t, where, its_core):
        pltpu.make_async_remote_copy(
            src_ref=part_send.at[t], dst_ref=part_recv.at[t // 2 * 2 + core],
            send_sem=pa_send, recv_sem=pa_recv, device_id=where, device_id_type=MESH).start()

    to_all(send_stats)
    stat_recv[pl.ds(core * pairs, 1)] = stat_send[pl.ds(core, 1)]

    for h in range(group):
        v_locals[h].wait()
        v_cross[h].wait_recv()
    for h in range(group):
        summed = jnp.dot(expos[h], v_buf[h], preferred_element_type=jnp.float32)
        for side in range(2):
            for part in range(2):
                part_wide[pl.ds(part * maps + 2 * h + side, tall, stride=2 * maps), :] = summed[
                    side * tall : (side + 1) * tall, part * 128 : part * 128 + 128]
    part_send[...] = part_wide[...].reshape(tall, 2 * maps, 128).astype(jnp.bfloat16)
    to_all(send_part)
    part_recv[core] = part_send[core]

    all_of(stat_recv.at[pl.ds(1, tall - 1)], st_recv)
    turned = stat_recv[...].T
    tops, totals = turned[0:maps], turned[maps : 2 * maps]

    def per_group(array, reduce, fill):
        zero = reduce(jnp.where(low, array, fill), axis=1, keepdims=True)
        one = reduce(jnp.where(low, fill, array), axis=1, keepdims=True)
        return jnp.where(low, zero, one)

    factor = jnp.exp(tops - per_group(tops, jnp.max, -3e38))
    factor = factor * sign / per_group(factor * totals, jnp.sum, 0.0)

    all_of(part_recv.at[pl.ds(1, tall - 1)], pa_recv)
    sums = [[jnp.zeros((maps, 128), jnp.float32) for _ in range(2)] for _ in range(2)]
    for s in range(pairs):
        for g in range(2):
            weight = factor[:, g * pairs + s : g * pairs + s + 1]
            block = part_recv[2 * s + g].astype(jnp.float32)
            for part in range(2):
                sums[part][g] = sums[part][g] + weight * block[part * maps : (part + 1) * maps]
    diffs = []
    for part in range(2):
        for g in range(2):
            sum_pad[part, g * maps : (g + 1) * maps] = sums[part][g]
        diffs.append(
            sum_pad[part, pl.ds(0, heads, stride=2), :] + sum_pad[part, pl.ds(1, heads, stride=2), :])
    square = jnp.sum(diffs[0] * diffs[0] + diffs[1] * diffs[1], axis=1, keepdims=True) * (1.0 / 256)
    scale = jnp.sqrt(square + 1e-05)
    normed = [diffs[part] / scale for part in range(2)]
    line = jnp.concatenate([normed[part][h : h + 1] for h in range(heads) for part in range(2)], axis=1)
    out_ref[...] = line

    for h in range(group):
        k_cross[h].wait_send()
        v_cross[h].wait_send()
    all_of(q_in.at[pl.ds(1, tall - 1)], qa_send)
    all_of(stat_send.at[pl.ds(1, tall - 1)], st_send)
    all_of(part_send.at[pl.ds(1, tall - 1)], pa_send)


def shards(queries, key_maps, values, lambdas, norm_gain):
    rows, cols = lax.axis_size("qrow"), lax.axis_size("kcol")
    heads = lambdas.shape[0]
    key_dev = key_maps.shape[0]
    assert queries.shape[0] == 1 and heads == 8
    assert key_maps.shape[1] == 2048 and values.shape[1] == 2048
    assert cols % 2 == 0 and rows * cols <= 2 * key_dev
    group = heads // 2
    maps = 2 * group
    pairs = rows * cols // 2
    tall = 2 * pairs
    f32, bf16 = jnp.float32, jnp.bfloat16
    dma = pltpu.SemaphoreType.DMA
    in_hbm = pl.BlockSpec(memory_space=pltpu.HBM)
    out = pl.pallas_call(
        functools.partial(kernel, rows, cols, key_dev, heads),
        out_shape=jax.ShapeDtypeStruct((1, 2048), f32),
        in_specs=[in_hbm] * 4,
        out_specs=pl.BlockSpec(memory_space=pltpu.VMEM),
        scratch_shapes=[
            pltpu.VMEM((1, 2048), bf16),
            pltpu.SMEM((heads,), f32),
            pltpu.VMEM((group, 2 * key_dev, 256), bf16),
            pltpu.VMEM((group, 2 * key_dev, 256), bf16),
            pltpu.VMEM((2, maps, 128), f32),
            pltpu.VMEM((2, maps, 128), bf16),
            pltpu.VMEM((tall, maps, 128), bf16),
            pltpu.VMEM((tall * maps, 128), f32),
            pltpu.VMEM((2 * tall, 2 * key_dev), f32),
            pltpu.VMEM((tall, 128), f32),
            pltpu.VMEM((tall, 128), f32),
            pltpu.VMEM((tall * 2 * maps, 128), f32),
            pltpu.VMEM((tall, 2 * maps, 128), bf16),
            pltpu.VMEM((tall, 2 * maps, 128), bf16),
            pltpu.VMEM((2, 2 * maps, 128), f32),
            dma, dma,
            dma((group,)), dma((group,)), dma((group,)), dma((group,)), dma((group,)), dma((group,)),
            dma, dma, dma, dma, dma, dma,
        ],
        compiler_params=pltpu.CompilerParams(
            collective_id=0, has_side_effects=True, vmem_limit_bytes=53 * 2**20),
        cost_estimate=pl.CostEstimate(
            flops=6 * tall * 2 * key_dev * 1024, bytes_accessed=4 * key_dev * 2048, transcendentals=0),
    )(queries, key_maps, values, lambdas)
    return (out * norm_gain[None, :]).astype(bf16)


def solution(mesh):
    in_specs = (
        P(("qrow", "kcol"), None),
        P(("qrow", "kcol"), None),
        P(("qrow", "kcol"), None),
        P(),
        P(),
    )
    out_specs = P(("qrow", "kcol"), None)
    return jax.shard_map(shards, mesh=mesh, in_specs=in_specs, out_specs=out_specs, check_vma=False)
```

```python
import functools
import math

import jax
import jax.numpy as jnp
from jax import lax
from jax.experimental import pallas as pl
from jax.experimental.pallas import tpu as pltpu
from jax.sharding import PartitionSpec as P

MESH = pl.DeviceIdType.MESH
LOWEST = -1e30


def kernel(
    rows, cols, key_dev, heads,
    q_hbm, k_hbm, v_hbm, lam_hbm,
    out_ref,
    q_own, lam_own, k_buf, v_buf, q_split, q_msg, q_in, q_wide, bias,
    stat_send, stat_recv, part_wide, part_send, part_recv, sum_pad,
    q_sem, lam_sem, k_own_sem, v_own_sem, k_send, k_recv, v_send, v_recv,
    qa_send, qa_recv, st_send, st_recv, pa_send, pa_recv,
):
    row = lax.axis_index("qrow")
    col = lax.axis_index("kcol")
    core = lax.rem(col, 2)
    half_cols = cols // 2
    pairs = rows * half_cols
    pair = row * half_cols + lax.div(col, 2)
    sib = (row, col + 1 - 2 * core)
    group = heads // 2
    maps = 2 * group
    width = group * 256
    tall = 2 * pairs
    keys = 2 * key_dev

    def peer(offset, its_core):
        other = pair + offset
        other = jnp.where(other >= pairs, other - pairs, other)
        its_row = lax.div(other, half_cols)
        return (its_row, 2 * (other - its_row * half_cols) + its_core)

    def for_peers(step):
        if pairs <= 16:
            for i in range(1, pairs):
                step(i)
        else:
            lax.fori_loop(1, pairs, lambda i, carry: (step(i), carry)[1], 0)

    def columns(which, h):
        return pl.ds(pl.multiple_of(which * width + h * 256, 128), 256)

    def all_of(ref, sem):
        pltpu.make_async_copy(ref, ref, sem).wait()

    q_copy = pltpu.make_async_copy(q_hbm, q_own, q_sem)
    q_copy.start()
    barrier = pltpu.get_barrier_semaphore()

    def greet(i):
        for j in range(2):
            pl.semaphore_signal(barrier, inc=1, device_id=peer(i, j), device_id_type=MESH)

    pl.semaphore_signal(barrier, inc=1, device_id=sib, device_id_type=MESH)
    for_peers(greet)

    lam_copy = pltpu.make_async_copy(lam_hbm, lam_own, lam_sem)
    lam_copy.start()
    k_locals, v_locals = [], []
    for h in range(group):
        k_locals.append(pltpu.make_async_copy(
            k_hbm.at[:, columns(core, h)], k_buf.at[h, pl.ds(0, key_dev)], k_own_sem.at[h]))
        k_locals[-1].start()
    for h in range(group):
        v_locals.append(pltpu.make_async_copy(
            v_hbm.at[:, columns(core, h)], v_buf.at[h, pl.ds(0, key_dev)], v_own_sem.at[h]))
        v_locals[-1].start()

    q_copy.wait()
    for g in range(2):
        for m in range(maps):
            at = (g * maps + m) * 128
            q_split[g, m : m + 1, :] = q_own[:, at : at + 128].astype(jnp.float32)

    q_msg[...] = q_split[...].astype(jnp.bfloat16)

    def to_all(send):
        for_peers(lambda i: [send(2 * i + j, peer(i, j), j) for j in range(2)])
        send(1 - core, sib, 1 - core)

    def send_query(t, where, its_core):
        back = lax.rem(tall - (t - its_core), tall) + core
        pltpu.make_async_remote_copy(
            src_ref=q_msg.at[its_core], dst_ref=q_in.at[back],
            send_sem=qa_send, recv_sem=qa_recv, device_id=where, device_id_type=MESH).start()

    pl.semaphore_wait(barrier, tall - 1)

    to_all(send_query)
    q_in[core] = q_msg[core]
    k_cross, v_cross = [], []
    for h in range(group):
        k_cross.append(pltpu.make_async_remote_copy(
            src_ref=k_hbm.at[:, columns(1 - core, h)], dst_ref=k_buf.at[h, pl.ds(key_dev, key_dev)],
            send_sem=k_send.at[h], recv_sem=k_recv.at[h], device_id=sib, device_id_type=MESH))
        k_cross[-1].start()

    for h in range(group):
        v_cross.append(pltpu.make_async_remote_copy(
            src_ref=v_hbm.at[:, columns(1 - core, h)], dst_ref=v_buf.at[h, pl.ds(key_dev, key_dev)],
            send_sem=v_send.at[h], recv_sem=v_recv.at[h], device_id=sib, device_id_type=MESH))
        v_cross[-1].start()

    lam_copy.wait()
    map_of = lax.broadcasted_iota(jnp.int32, (maps, tall), 0)
    low = lax.broadcasted_iota(jnp.int32, (maps, tall), 1) < pairs
    sign = jnp.ones((maps, tall), jnp.float32)
    for h in range(group):
        sign = jnp.where(map_of == 2 * h + 1, jnp.where(low, -lam_own[h], -lam_own[group + h]), sign)

    row_of = lax.broadcasted_iota(jnp.int32, (2 * tall, keys), 0)
    col_of = lax.broadcasted_iota(jnp.int32, (2 * tall, keys), 1)
    query = 2 * pair + jnp.where(row_of < tall, row_of, row_of - tall)
    query = jnp.where(query >= tall, query - tall, query)
    place = jnp.where(
        col_of < key_dev,
        (2 * pair + core) * key_dev + col_of,
        (2 * pair + 1 - core) * key_dev + col_of - key_dev)
    bias[...] = jnp.where(place <= tall * key_dev - tall + query, 0.0, LOWEST)
    lane = lax.broadcasted_iota(jnp.int32, (tall, 128), 1)
    scaling = 1.0 / math.sqrt(128)

    for h in range(group):
        k_locals[h].wait()
        k_cross[h].wait_recv()
    all_of(q_in.at[pl.ds(1, tall - 1)], qa_recv)
    q_wide[...] = q_in[...].astype(jnp.float32).reshape(tall * maps, 128)

    stats = jnp.zeros((tall, 128), jnp.float32)
    expos = []
    blank = jnp.zeros((tall, 128), jnp.bfloat16)
    for h in range(group):
        first = q_wide[pl.ds(2 * h, tall, stride=maps), :].astype(jnp.bfloat16)
        second = q_wide[pl.ds(2 * h + 1, tall, stride=maps), :].astype(jnp.bfloat16)
        both = jnp.concatenate(
            [jnp.concatenate([first, blank], axis=1), jnp.concatenate([blank, second], axis=1)], axis=0)
        score = lax.dot_general(
            both, k_buf[h], (((1,), (1,)), ((), ())), preferred_element_type=jnp.float32)
        score = score * scaling + bias[...]
        top = jnp.max(score, axis=1, keepdims=True)
        expo = jnp.exp(score - top)
        total = jnp.sum(expo, axis=1, keepdims=True)
        for side in range(2):
            m = 2 * h + side
            at = slice(side * tall, (side + 1) * tall)
            stats = jnp.where(lane == m, top[at], jnp.where(lane == maps + m, total[at], stats))
        expos.append(expo.astype(jnp.bfloat16))
    stat_send[...] = stats

    def send_stats(t, where, its_core):
        pltpu.make_async_remote_copy(
            src_ref=stat_send.at[pl.ds(t, 1)], dst_ref=stat_recv.at[pl.ds(core * pairs + t // 2, 1)],
            send_sem=st_send, recv_sem=st_recv, device_id=where, device_id_type=MESH).start()

    def send_part(t, where, its_core):
        pltpu.make_async_remote_copy(
            src_ref=part_send.at[t], dst_ref=part_recv.at[t // 2 * 2 + core],
            send_sem=pa_send, recv_sem=pa_recv, device_id=where, device_id_type=MESH).start()

    to_all(send_stats)
    stat_recv[pl.ds(core * pairs, 1)] = stat_send[pl.ds(core, 1)]

    for h in range(group):
        v_locals[h].wait()
        v_cross[h].wait_recv()
    for h in range(group):
        summed = jnp.dot(expos[h], v_buf[h], preferred_element_type=jnp.float32)
        for side in range(2):
            for part in range(2):
                part_wide[pl.ds(part * maps + 2 * h + side, tall, stride=2 * maps), :] = summed[
                    side * tall : (side + 1) * tall, part * 128 : part * 128 + 128]
    part_send[...] = part_wide[...].reshape(tall, 2 * maps, 128).astype(jnp.bfloat16)
    to_all(send_part)
    part_recv[core] = part_send[core]

    all_of(stat_recv.at[pl.ds(1, tall - 1)], st_recv)
    turned = stat_recv[...].T
    tops, totals = turned[0:maps], turned[maps : 2 * maps]

    def per_group(array, reduce, fill):
        zero = reduce(jnp.where(low, array, fill), axis=1, keepdims=True)
        one = reduce(jnp.where(low, fill, array), axis=1, keepdims=True)
        return jnp.where(low, zero, one)

    factor = jnp.exp(tops - per_group(tops, jnp.max, -3e38))
    factor = factor * sign / per_group(factor * totals, jnp.sum, 0.0)

    all_of(part_recv.at[pl.ds(1, tall - 1)], pa_recv)
    sums = [[jnp.zeros((maps, 128), jnp.float32) for _ in range(2)] for _ in range(2)]
    for s in range(pairs):
        for g in range(2):
            weight = factor[:, g * pairs + s : g * pairs + s + 1]
            block = part_recv[2 * s + g].astype(jnp.float32)
            for part in range(2):
                sums[part][g] = sums[part][g] + weight * block[part * maps : (part + 1) * maps]
    diffs = []
    for part in range(2):
        for g in range(2):
            sum_pad[part, g * maps : (g + 1) * maps] = sums[part][g]
        diffs.append(
            sum_pad[part, pl.ds(0, heads, stride=2), :] + sum_pad[part, pl.ds(1, heads, stride=2), :])
    square = jnp.sum(diffs[0] * diffs[0] + diffs[1] * diffs[1], axis=1, keepdims=True) * (1.0 / 256)
    scale = jnp.sqrt(square + 1e-05)
    normed = [diffs[part] / scale for part in range(2)]
    line = jnp.concatenate([normed[part][h : h + 1] for h in range(heads) for part in range(2)], axis=1)
    out_ref[...] = line

    for h in range(group):
        k_cross[h].wait_send()
        v_cross[h].wait_send()
    all_of(q_in.at[pl.ds(1, tall - 1)], qa_send)
    all_of(stat_send.at[pl.ds(1, tall - 1)], st_send)
    all_of(part_send.at[pl.ds(1, tall - 1)], pa_send)


def shards(queries, key_maps, values, lambdas, norm_gain):
    rows, cols = lax.axis_size("qrow"), lax.axis_size("kcol")
    heads = lambdas.shape[0]
    key_dev = key_maps.shape[0]
    assert queries.shape[0] == 1 and heads == 8
    assert key_maps.shape[1] == 2048 and values.shape[1] == 2048
    assert cols % 2 == 0 and rows * cols <= 2 * key_dev
    group = heads // 2
    maps = 2 * group
    pairs = rows * cols // 2
    tall = 2 * pairs
    f32, bf16 = jnp.float32, jnp.bfloat16
    dma = pltpu.SemaphoreType.DMA
    in_hbm = pl.BlockSpec(memory_space=pltpu.HBM)
    out = pl.pallas_call(
        functools.partial(kernel, rows, cols, key_dev, heads),
        out_shape=jax.ShapeDtypeStruct((1, 2048), f32),
        in_specs=[in_hbm] * 4,
        out_specs=pl.BlockSpec(memory_space=pltpu.VMEM),
        scratch_shapes=[
            pltpu.VMEM((1, 2048), bf16),
            pltpu.SMEM((heads,), f32),
            pltpu.VMEM((group, 2 * key_dev, 256), bf16),
            pltpu.VMEM((group, 2 * key_dev, 256), bf16),
            pltpu.VMEM((2, maps, 128), f32),
            pltpu.VMEM((2, maps, 128), bf16),
            pltpu.VMEM((tall, maps, 128), bf16),
            pltpu.VMEM((tall * maps, 128), f32),
            pltpu.VMEM((2 * tall, 2 * key_dev), f32),
            pltpu.VMEM((tall, 128), f32),
            pltpu.VMEM((tall, 128), f32),
            pltpu.VMEM((tall * 2 * maps, 128), f32),
            pltpu.VMEM((tall, 2 * maps, 128), bf16),
            pltpu.VMEM((tall, 2 * maps, 128), bf16),
            pltpu.VMEM((2, 2 * maps, 128), f32),
            dma, dma,
            dma((group,)), dma((group,)), dma((group,)), dma((group,)), dma((group,)), dma((group,)),
            dma, dma, dma, dma, dma, dma,
        ],
        compiler_params=pltpu.CompilerParams(
            collective_id=0, has_side_effects=True, vmem_limit_bytes=54 * 2**20 - 80 * 2**10),
        cost_estimate=pl.CostEstimate(
            flops=6 * tall * 2 * key_dev * 1024, bytes_accessed=4 * key_dev * 2048, transcendentals=0),
    )(queries, key_maps, values, lambdas)
    return (out * norm_gain[None, :]).astype(bf16)


def solution(mesh):
    in_specs = (
        P(("qrow", "kcol"), None),
        P(("qrow", "kcol"), None),
        P(("qrow", "kcol"), None),
        P(),
        P(),
    )
    out_specs = P(("qrow", "kcol"), None)
    return jax.shard_map(shards, mesh=mesh, in_specs=in_specs, out_specs=out_specs, check_vma=False)
```

```python
import functools
import math

import jax
import jax.numpy as jnp
from jax import lax
from jax.experimental import pallas as pl
from jax.experimental.pallas import tpu as pltpu
from jax.sharding import PartitionSpec as P

MESH = pl.DeviceIdType.MESH
LOWEST = -1e30


def kernel(
    rows, cols, key_dev, heads,
    q_hbm, k_hbm, v_hbm, lam_hbm,
    out_ref,
    q_own, lam_own, k_buf, v_buf, q_split, q_msg, q_in, q_wide, bias,
    stat_send, stat_recv, part_wide, part_send, part_recv, sum_pad,
    q_sem, lam_sem, k_own_sem, v_own_sem, k_send, k_recv, v_send, v_recv,
    qa_send, qa_recv, st_send, st_recv, pa_send, pa_recv,
):
    row = lax.axis_index("qrow")
    col = lax.axis_index("kcol")
    core = lax.rem(col, 2)
    half_cols = cols // 2
    pairs = rows * half_cols
    pair = row * half_cols + lax.div(col, 2)
    sib = (row, col + 1 - 2 * core)
    group = heads // 2
    maps = 2 * group
    width = group * 256
    tall = 2 * pairs
    keys = 2 * key_dev

    def peer(offset, its_core):
        other = pair + offset
        other = jnp.where(other >= pairs, other - pairs, other)
        its_row = lax.div(other, half_cols)
        return (its_row, 2 * (other - its_row * half_cols) + its_core)

    def for_peers(step, first=1, last=pairs):
        if pairs <= 16:
            for i in range(first, last):
                step(i)
        else:
            lax.fori_loop(first, last, lambda i, carry: (step(i), carry)[1], 0)

    def columns(which, h):
        return pl.ds(pl.multiple_of(which * width + h * 256, 128), 256)

    def all_of(ref, sem):
        pltpu.make_async_copy(ref, ref, sem).wait()

    q_copy = pltpu.make_async_copy(q_hbm, q_own, q_sem)
    q_copy.start()
    barrier = pltpu.get_barrier_semaphore()

    def greet(i):
        for j in range(2):
            pl.semaphore_signal(barrier, inc=1, device_id=peer(i, j), device_id_type=MESH)

    pl.semaphore_signal(barrier, inc=1, device_id=sib, device_id_type=MESH)
    for_peers(greet)

    lam_copy = pltpu.make_async_copy(lam_hbm, lam_own, lam_sem)
    lam_copy.start()
    k_locals, v_locals = [], []
    for h in range(group):
        k_locals.append(pltpu.make_async_copy(
            k_hbm.at[:, columns(core, h)], k_buf.at[h, pl.ds(0, key_dev)], k_own_sem.at[h]))
        k_locals[-1].start()
    for h in range(group):
        v_locals.append(pltpu.make_async_copy(
            v_hbm.at[:, columns(core, h)], v_buf.at[h, pl.ds(0, key_dev)], v_own_sem.at[h]))
        v_locals[-1].start()

    q_copy.wait()
    for g in range(2):
        for m in range(maps):
            at = (g * maps + m) * 128
            q_split[g, m : m + 1, :] = q_own[:, at : at + 128].astype(jnp.float32)

    q_msg[...] = q_split[...].astype(jnp.bfloat16)

    def to_all(send):
        for_peers(lambda i: [send(2 * i + j, peer(i, j), j) for j in range(2)])
        send(1 - core, sib, 1 - core)

    def send_query(t, where, its_core):
        back = lax.rem(tall - (t - its_core), tall) + core
        pltpu.make_async_remote_copy(
            src_ref=q_msg.at[its_core], dst_ref=q_in.at[back],
            send_sem=qa_send, recv_sem=qa_recv, device_id=where, device_id_type=MESH).start()

    pl.semaphore_wait(barrier, tall - 1)

    to_all(send_query)
    q_in[core] = q_msg[core]
    k_cross, v_cross = [], []
    for h in range(group):
        k_cross.append(pltpu.make_async_remote_copy(
            src_ref=k_hbm.at[:, columns(1 - core, h)], dst_ref=k_buf.at[h, pl.ds(key_dev, key_dev)],
            send_sem=k_send.at[h], recv_sem=k_recv.at[h], device_id=sib, device_id_type=MESH))
        k_cross[-1].start()

    for h in range(group):
        v_cross.append(pltpu.make_async_remote_copy(
            src_ref=v_hbm.at[:, columns(1 - core, h)], dst_ref=v_buf.at[h, pl.ds(key_dev, key_dev)],
            send_sem=v_send.at[h], recv_sem=v_recv.at[h], device_id=sib, device_id_type=MESH))
        v_cross[-1].start()

    lam_copy.wait()
    map_of = lax.broadcasted_iota(jnp.int32, (maps, tall), 0)
    low = lax.broadcasted_iota(jnp.int32, (maps, tall), 1) < pairs
    sign = jnp.ones((maps, tall), jnp.float32)
    for h in range(group):
        sign = jnp.where(map_of == 2 * h + 1, jnp.where(low, -lam_own[h], -lam_own[group + h]), sign)

    row_of = lax.broadcasted_iota(jnp.int32, (2 * tall, keys), 0)
    col_of = lax.broadcasted_iota(jnp.int32, (2 * tall, keys), 1)
    query = 2 * pair + jnp.where(row_of < tall, row_of, row_of - tall)
    query = jnp.where(query >= tall, query - tall, query)
    place = jnp.where(
        col_of < key_dev,
        (2 * pair + core) * key_dev + col_of,
        (2 * pair + 1 - core) * key_dev + col_of - key_dev)
    bias[...] = jnp.where(place <= tall * key_dev - tall + query, 0.0, LOWEST)
    lane = lax.broadcasted_iota(jnp.int32, (tall, 128), 1)
    scaling = 1.0 / math.sqrt(128)

    for h in range(group):
        k_locals[h].wait()
        k_cross[h].wait_recv()
    all_of(q_in.at[pl.ds(1, tall - 1)], qa_recv)
    q_wide[...] = q_in[...].astype(jnp.float32).reshape(tall * maps, 128)

    stats = jnp.zeros((tall, 128), jnp.float32)
    expos = []
    blank = jnp.zeros((tall, 128), jnp.bfloat16)
    for h in range(group):
        first = q_wide[pl.ds(2 * h, tall, stride=maps), :].astype(jnp.bfloat16)
        second = q_wide[pl.ds(2 * h + 1, tall, stride=maps), :].astype(jnp.bfloat16)
        both = jnp.concatenate(
            [jnp.concatenate([first, blank], axis=1), jnp.concatenate([blank, second], axis=1)], axis=0)
        score = lax.dot_general(
            both, k_buf[h], (((1,), (1,)), ((), ())), preferred_element_type=jnp.float32)
        score = score * scaling + bias[...]
        top = jnp.max(score, axis=1, keepdims=True)
        expo = jnp.exp(score - top)
        total = jnp.sum(expo, axis=1, keepdims=True)
        for side in range(2):
            m = 2 * h + side
            at = slice(side * tall, (side + 1) * tall)
            stats = jnp.where(lane == m, top[at], jnp.where(lane == maps + m, total[at], stats))
        expos.append(expo.astype(jnp.bfloat16))
    stat_send[...] = stats

    def send_stats(t, where, its_core):
        pltpu.make_async_remote_copy(
            src_ref=stat_send.at[pl.ds(t, 1)], dst_ref=stat_recv.at[pl.ds(core * pairs + t // 2, 1)],
            send_sem=st_send, recv_sem=st_recv, device_id=where, device_id_type=MESH).start()

    def send_part(t, where, its_core):
        pltpu.make_async_remote_copy(
            src_ref=part_send.at[t], dst_ref=part_recv.at[t // 2 * 2 + core],
            send_sem=pa_send, recv_sem=pa_recv, device_id=where, device_id_type=MESH).start()

    to_all(send_stats)
    stat_recv[pl.ds(core * pairs, 1)] = stat_send[pl.ds(core, 1)]

    for h in range(group):
        v_locals[h].wait()
        v_cross[h].wait_recv()
    def weigh(start):
        for h in range(group):
            weights = jnp.concatenate(
                [expos[h][start : start + pairs], expos[h][tall + start : tall + start + pairs]], axis=0)
            summed = jnp.dot(weights, v_buf[h], preferred_element_type=jnp.float32)
            for side in range(2):
                for part in range(2):
                    at = pl.ds(start * 2 * maps + part * maps + 2 * h + side, pairs, stride=2 * maps)
                    part_wide[at, :] = summed[side * pairs : (side + 1) * pairs, part * 128 : part * 128 + 128]
        part_send[start : start + pairs] = part_wide[start * 2 * maps : (start + pairs) * 2 * maps].reshape(
            pairs, 2 * maps, 128).astype(jnp.bfloat16)

    middle = pairs // 2
    weigh(0)
    for_peers(lambda i: [send_part(2 * i + j, peer(i, j), j) for j in range(2)], 1, middle)
    weigh(pairs)
    for_peers(lambda i: [send_part(2 * i + j, peer(i, j), j) for j in range(2)], middle, pairs)
    send_part(1 - core, sib, 1 - core)
    part_recv[core] = part_send[core]

    all_of(stat_recv.at[pl.ds(1, tall - 1)], st_recv)
    turned = stat_recv[...].T
    tops, totals = turned[0:maps], turned[maps : 2 * maps]

    def per_group(array, reduce, fill):
        zero = reduce(jnp.where(low, array, fill), axis=1, keepdims=True)
        one = reduce(jnp.where(low, fill, array), axis=1, keepdims=True)
        return jnp.where(low, zero, one)

    factor = jnp.exp(tops - per_group(tops, jnp.max, -3e38))
    factor = factor * sign / per_group(factor * totals, jnp.sum, 0.0)

    all_of(part_recv.at[pl.ds(1, tall - 1)], pa_recv)
    sums = [[jnp.zeros((maps, 128), jnp.float32) for _ in range(2)] for _ in range(2)]
    for s in range(pairs):
        for g in range(2):
            weight = factor[:, g * pairs + s : g * pairs + s + 1]
            block = part_recv[2 * s + g].astype(jnp.float32)
            for part in range(2):
                sums[part][g] = sums[part][g] + weight * block[part * maps : (part + 1) * maps]
    diffs = []
    for part in range(2):
        for g in range(2):
            sum_pad[part, g * maps : (g + 1) * maps] = sums[part][g]
        diffs.append(
            sum_pad[part, pl.ds(0, heads, stride=2), :] + sum_pad[part, pl.ds(1, heads, stride=2), :])
    square = jnp.sum(diffs[0] * diffs[0] + diffs[1] * diffs[1], axis=1, keepdims=True) * (1.0 / 256)
    scale = jnp.sqrt(square + 1e-05)
    normed = [diffs[part] / scale for part in range(2)]
    line = jnp.concatenate([normed[part][h : h + 1] for h in range(heads) for part in range(2)], axis=1)
    out_ref[...] = line

    for h in range(group):
        k_cross[h].wait_send()
        v_cross[h].wait_send()
    all_of(q_in.at[pl.ds(1, tall - 1)], qa_send)
    all_of(stat_send.at[pl.ds(1, tall - 1)], st_send)
    all_of(part_send.at[pl.ds(1, tall - 1)], pa_send)


def shards(queries, key_maps, values, lambdas, norm_gain):
    rows, cols = lax.axis_size("qrow"), lax.axis_size("kcol")
    heads = lambdas.shape[0]
    key_dev = key_maps.shape[0]
    assert queries.shape[0] == 1 and heads == 8
    assert key_maps.shape[1] == 2048 and values.shape[1] == 2048
    assert cols % 2 == 0 and rows * cols <= 2 * key_dev
    group = heads // 2
    maps = 2 * group
    pairs = rows * cols // 2
    tall = 2 * pairs
    f32, bf16 = jnp.float32, jnp.bfloat16
    dma = pltpu.SemaphoreType.DMA
    in_hbm = pl.BlockSpec(memory_space=pltpu.HBM)
    out = pl.pallas_call(
        functools.partial(kernel, rows, cols, key_dev, heads),
        out_shape=jax.ShapeDtypeStruct((1, 2048), f32),
        in_specs=[in_hbm] * 4,
        out_specs=pl.BlockSpec(memory_space=pltpu.VMEM),
        scratch_shapes=[
            pltpu.VMEM((1, 2048), bf16),
            pltpu.SMEM((heads,), f32),
            pltpu.VMEM((group, 2 * key_dev, 256), bf16),
            pltpu.VMEM((group, 2 * key_dev, 256), bf16),
            pltpu.VMEM((2, maps, 128), f32),
            pltpu.VMEM((2, maps, 128), bf16),
            pltpu.VMEM((tall, maps, 128), bf16),
            pltpu.VMEM((tall * maps, 128), f32),
            pltpu.VMEM((2 * tall, 2 * key_dev), f32),
            pltpu.VMEM((tall, 128), f32),
            pltpu.VMEM((tall, 128), f32),
            pltpu.VMEM((tall * 2 * maps, 128), f32),
            pltpu.VMEM((tall, 2 * maps, 128), bf16),
            pltpu.VMEM((tall, 2 * maps, 128), bf16),
            pltpu.VMEM((2, 2 * maps, 128), f32),
            dma, dma,
            dma((group,)), dma((group,)), dma((group,)), dma((group,)), dma((group,)), dma((group,)),
            dma, dma, dma, dma, dma, dma,
        ],
        compiler_params=pltpu.CompilerParams(
            collective_id=0, has_side_effects=True, vmem_limit_bytes=54 * 2**20 - 80 * 2**10),
        cost_estimate=pl.CostEstimate(
            flops=6 * tall * 2 * key_dev * 1024, bytes_accessed=4 * key_dev * 2048, transcendentals=0),
    )(queries, key_maps, values, lambdas)
    return (out * norm_gain[None, :]).astype(bf16)


def solution(mesh):
    in_specs = (
        P(("qrow", "kcol"), None),
        P(("qrow", "kcol"), None),
        P(("qrow", "kcol"), None),
        P(),
        P(),
    )
    out_specs = P(("qrow", "kcol"), None)
    return jax.shard_map(shards, mesh=mesh, in_specs=in_specs, out_specs=out_specs, check_vma=False)
```

```python
import functools
import math

import jax
import jax.numpy as jnp
from jax import lax
from jax.experimental import pallas as pl
from jax.experimental.pallas import tpu as pltpu
from jax.sharding import PartitionSpec as P

MESH = pl.DeviceIdType.MESH
LOWEST = -1e30


def kernel(
    rows, cols, key_dev, heads,
    q_hbm, k_hbm, v_hbm, lam_hbm,
    out_ref,
    q_own, lam_own, k_buf, v_buf, q_split, q_msg, q_in, q_wide, bias,
    stat_send, stat_recv, part_wide, part_send, part_recv, sum_pad,
    q_sem, lam_sem, k_own_sem, v_own_sem, k_send, k_recv, v_send, v_recv,
    qa_send, qa_recv, st_send, st_recv, pa_send, pa_recv,
):
    row = lax.axis_index("qrow")
    col = lax.axis_index("kcol")
    core = lax.rem(col, 2)
    half_cols = cols // 2
    pairs = rows * half_cols
    pair = row * half_cols + lax.div(col, 2)
    sib = (row, col + 1 - 2 * core)
    group = heads // 2
    maps = 2 * group
    width = group * 256
    tall = 2 * pairs
    keys = 2 * key_dev

    def peer(offset, its_core):
        other = pair + offset
        other = jnp.where(other >= pairs, other - pairs, other)
        its_row = lax.div(other, half_cols)
        return (its_row, 2 * (other - its_row * half_cols) + its_core)

    def for_peers(step, first=1, last=pairs):
        if pairs <= 16:
            for i in range(first, last):
                step(i)
        else:
            lax.fori_loop(first, last, lambda i, carry: (step(i), carry)[1], 0)

    def columns(which, h):
        return pl.ds(pl.multiple_of(which * width + h * 256, 128), 256)

    def all_of(ref, sem):
        pltpu.make_async_copy(ref, ref, sem).wait()

    q_copy = pltpu.make_async_copy(q_hbm, q_own, q_sem)
    q_copy.start()
    barrier = pltpu.get_barrier_semaphore()

    def greet(i):
        for j in range(2):
            pl.semaphore_signal(barrier, inc=1, device_id=peer(i, j), device_id_type=MESH)

    pl.semaphore_signal(barrier, inc=1, device_id=sib, device_id_type=MESH)
    for_peers(greet)

    lam_copy = pltpu.make_async_copy(lam_hbm, lam_own, lam_sem)
    lam_copy.start()
    k_locals, v_locals = [], []
    for h in range(group):
        k_locals.append(pltpu.make_async_copy(
            k_hbm.at[:, columns(core, h)], k_buf.at[h, pl.ds(0, key_dev)], k_own_sem.at[h]))
        k_locals[-1].start()
    for h in range(group):
        v_locals.append(pltpu.make_async_copy(
            v_hbm.at[:, columns(core, h)], v_buf.at[h, pl.ds(0, key_dev)], v_own_sem.at[h]))
        v_locals[-1].start()

    q_copy.wait()
    for g in range(2):
        for m in range(maps):
            at = (g * maps + m) * 128
            q_split[g, m : m + 1, :] = q_own[:, at : at + 128].astype(jnp.float32)

    q_msg[...] = q_split[...].astype(jnp.bfloat16)

    def to_all(send):
        for_peers(lambda i: [send(2 * i + j, peer(i, j), j) for j in range(2)])
        send(1 - core, sib, 1 - core)

    def send_query(t, where, its_core):
        back = lax.rem(tall - (t - its_core), tall) + core
        pltpu.make_async_remote_copy(
            src_ref=q_msg.at[its_core], dst_ref=q_in.at[back],
            send_sem=qa_send, recv_sem=qa_recv, device_id=where, device_id_type=MESH).start()

    pl.semaphore_wait(barrier, tall - 1)

    to_all(send_query)
    q_in[core] = q_msg[core]
    k_cross, v_cross = [], []
    for h in range(group):
        k_cross.append(pltpu.make_async_remote_copy(
            src_ref=k_hbm.at[:, columns(1 - core, h)], dst_ref=k_buf.at[h, pl.ds(key_dev, key_dev)],
            send_sem=k_send.at[h], recv_sem=k_recv.at[h], device_id=sib, device_id_type=MESH))
        k_cross[-1].start()

    for h in range(group):
        v_cross.append(pltpu.make_async_remote_copy(
            src_ref=v_hbm.at[:, columns(1 - core, h)], dst_ref=v_buf.at[h, pl.ds(key_dev, key_dev)],
            send_sem=v_send.at[h], recv_sem=v_recv.at[h], device_id=sib, device_id_type=MESH))
        v_cross[-1].start()

    lam_copy.wait()
    map_of = lax.broadcasted_iota(jnp.int32, (maps, tall), 0)
    low = lax.broadcasted_iota(jnp.int32, (maps, tall), 1) < pairs
    sign = jnp.ones((maps, tall), jnp.float32)
    for h in range(group):
        sign = jnp.where(map_of == 2 * h + 1, jnp.where(low, -lam_own[h], -lam_own[group + h]), sign)

    row_of = lax.broadcasted_iota(jnp.int32, (2 * tall, keys), 0)
    col_of = lax.broadcasted_iota(jnp.int32, (2 * tall, keys), 1)
    query = 2 * pair + jnp.where(row_of < tall, row_of, row_of - tall)
    query = jnp.where(query >= tall, query - tall, query)
    place = jnp.where(
        col_of < key_dev,
        (2 * pair + core) * key_dev + col_of,
        (2 * pair + 1 - core) * key_dev + col_of - key_dev)
    bias[...] = jnp.where(place <= tall * key_dev - tall + query, 0.0, LOWEST)
    lane = lax.broadcasted_iota(jnp.int32, (tall, 128), 1)
    scaling = 1.0 / math.sqrt(128)

    for h in range(group):
        k_locals[h].wait()
        k_cross[h].wait_recv()
    all_of(q_in.at[pl.ds(1, tall - 1)], qa_recv)
    q_wide[...] = q_in[...].astype(jnp.float32).reshape(tall * maps, 128)

    stats = jnp.zeros((tall, 128), jnp.float32)
    expos = []
    blank = jnp.zeros((tall, 128), jnp.bfloat16)
    for h in range(group):
        first = q_wide[pl.ds(2 * h, tall, stride=maps), :].astype(jnp.bfloat16)
        second = q_wide[pl.ds(2 * h + 1, tall, stride=maps), :].astype(jnp.bfloat16)
        both = jnp.concatenate(
            [jnp.concatenate([first, blank], axis=1), jnp.concatenate([blank, second], axis=1)], axis=0)
        score = lax.dot_general(
            both, k_buf[h], (((1,), (1,)), ((), ())), preferred_element_type=jnp.float32)
        score = score * scaling + bias[...]
        top = jnp.max(score, axis=1, keepdims=True)
        expo = jnp.exp(score - top)
        total = jnp.sum(expo, axis=1, keepdims=True)
        for side in range(2):
            m = 2 * h + side
            at = slice(side * tall, (side + 1) * tall)
            stats = jnp.where(lane == m, top[at], jnp.where(lane == maps + m, total[at], stats))
        expos.append(expo.astype(jnp.bfloat16))
    stat_send[...] = stats

    def send_stats(t, where, its_core):
        pltpu.make_async_remote_copy(
            src_ref=stat_send.at[pl.ds(t, 1)], dst_ref=stat_recv.at[pl.ds(core * pairs + t // 2, 1)],
            send_sem=st_send, recv_sem=st_recv, device_id=where, device_id_type=MESH).start()

    def send_part(t, where, its_core):
        pltpu.make_async_remote_copy(
            src_ref=part_send.at[t], dst_ref=part_recv.at[t // 2 * 2 + core],
            send_sem=pa_send, recv_sem=pa_recv, device_id=where, device_id_type=MESH).start()


    for h in range(group):
        v_locals[h].wait()
        v_cross[h].wait_recv()
    def weigh(start):
        for h in range(group):
            weights = jnp.concatenate(
                [expos[h][start : start + pairs], expos[h][tall + start : tall + start + pairs]], axis=0)
            summed = jnp.dot(weights, v_buf[h], preferred_element_type=jnp.float32)
            for side in range(2):
                for part in range(2):
                    at = pl.ds(start * 2 * maps + part * maps + 2 * h + side, pairs, stride=2 * maps)
                    part_wide[at, :] = summed[side * pairs : (side + 1) * pairs, part * 128 : part * 128 + 128]
        part_send[start : start + pairs] = part_wide[start * 2 * maps : (start + pairs) * 2 * maps].reshape(
            pairs, 2 * maps, 128).astype(jnp.bfloat16)

    middle = pairs // 2
    weigh(0)
    for_peers(lambda i: [send_part(2 * i + j, peer(i, j), j) for j in range(2)], 1, middle)
    to_all(send_stats)
    stat_recv[pl.ds(core * pairs, 1)] = stat_send[pl.ds(core, 1)]
    weigh(pairs)
    for_peers(lambda i: [send_part(2 * i + j, peer(i, j), j) for j in range(2)], middle, pairs)
    send_part(1 - core, sib, 1 - core)
    part_recv[core] = part_send[core]

    all_of(stat_recv.at[pl.ds(1, tall - 1)], st_recv)
    turned = stat_recv[...].T
    tops, totals = turned[0:maps], turned[maps : 2 * maps]

    def per_group(array, reduce, fill):
        zero = reduce(jnp.where(low, array, fill), axis=1, keepdims=True)
        one = reduce(jnp.where(low, fill, array), axis=1, keepdims=True)
        return jnp.where(low, zero, one)

    factor = jnp.exp(tops - per_group(tops, jnp.max, -3e38))
    factor = factor * sign / per_group(factor * totals, jnp.sum, 0.0)

    all_of(part_recv.at[pl.ds(1, tall - 1)], pa_recv)
    sums = [[jnp.zeros((maps, 128), jnp.float32) for _ in range(2)] for _ in range(2)]
    for s in range(pairs):
        for g in range(2):
            weight = factor[:, g * pairs + s : g * pairs + s + 1]
            block = part_recv[2 * s + g].astype(jnp.float32)
            for part in range(2):
                sums[part][g] = sums[part][g] + weight * block[part * maps : (part + 1) * maps]
    diffs = []
    for part in range(2):
        for g in range(2):
            sum_pad[part, g * maps : (g + 1) * maps] = sums[part][g]
        diffs.append(
            sum_pad[part, pl.ds(0, heads, stride=2), :] + sum_pad[part, pl.ds(1, heads, stride=2), :])
    square = jnp.sum(diffs[0] * diffs[0] + diffs[1] * diffs[1], axis=1, keepdims=True) * (1.0 / 256)
    scale = jnp.sqrt(square + 1e-05)
    normed = [diffs[part] / scale for part in range(2)]
    line = jnp.concatenate([normed[part][h : h + 1] for h in range(heads) for part in range(2)], axis=1)
    out_ref[...] = line

    for h in range(group):
        k_cross[h].wait_send()
        v_cross[h].wait_send()
    all_of(q_in.at[pl.ds(1, tall - 1)], qa_send)
    all_of(stat_send.at[pl.ds(1, tall - 1)], st_send)
    all_of(part_send.at[pl.ds(1, tall - 1)], pa_send)


def shards(queries, key_maps, values, lambdas, norm_gain):
    rows, cols = lax.axis_size("qrow"), lax.axis_size("kcol")
    heads = lambdas.shape[0]
    key_dev = key_maps.shape[0]
    assert queries.shape[0] == 1 and heads == 8
    assert key_maps.shape[1] == 2048 and values.shape[1] == 2048
    assert cols % 2 == 0 and rows * cols <= 2 * key_dev
    group = heads // 2
    maps = 2 * group
    pairs = rows * cols // 2
    tall = 2 * pairs
    f32, bf16 = jnp.float32, jnp.bfloat16
    dma = pltpu.SemaphoreType.DMA
    in_hbm = pl.BlockSpec(memory_space=pltpu.HBM)
    out = pl.pallas_call(
        functools.partial(kernel, rows, cols, key_dev, heads),
        out_shape=jax.ShapeDtypeStruct((1, 2048), f32),
        in_specs=[in_hbm] * 4,
        out_specs=pl.BlockSpec(memory_space=pltpu.VMEM),
        scratch_shapes=[
            pltpu.VMEM((1, 2048), bf16),
            pltpu.SMEM((heads,), f32),
            pltpu.VMEM((group, 2 * key_dev, 256), bf16),
            pltpu.VMEM((group, 2 * key_dev, 256), bf16),
            pltpu.VMEM((2, maps, 128), f32),
            pltpu.VMEM((2, maps, 128), bf16),
            pltpu.VMEM((tall, maps, 128), bf16),
            pltpu.VMEM((tall * maps, 128), f32),
            pltpu.VMEM((2 * tall, 2 * key_dev), f32),
            pltpu.VMEM((tall, 128), f32),
            pltpu.VMEM((tall, 128), f32),
            pltpu.VMEM((tall * 2 * maps, 128), f32),
            pltpu.VMEM((tall, 2 * maps, 128), bf16),
            pltpu.VMEM((tall, 2 * maps, 128), bf16),
            pltpu.VMEM((2, 2 * maps, 128), f32),
            dma, dma,
            dma((group,)), dma((group,)), dma((group,)), dma((group,)), dma((group,)), dma((group,)),
            dma, dma, dma, dma, dma, dma,
        ],
        compiler_params=pltpu.CompilerParams(
            collective_id=0, has_side_effects=True, vmem_limit_bytes=54 * 2**20 - 80 * 2**10),
        cost_estimate=pl.CostEstimate(
            flops=6 * tall * 2 * key_dev * 1024, bytes_accessed=4 * key_dev * 2048, transcendentals=0),
    )(queries, key_maps, values, lambdas)
    return (out * norm_gain[None, :]).astype(bf16)


def solution(mesh):
    in_specs = (
        P(("qrow", "kcol"), None),
        P(("qrow", "kcol"), None),
        P(("qrow", "kcol"), None),
        P(),
        P(),
    )
    out_specs = P(("qrow", "kcol"), None)
    return jax.shard_map(shards, mesh=mesh, in_specs=in_specs, out_specs=out_specs, check_vma=False)
```
